256 devices in a mesh: lat: 8 (over z), lon: 8 (over x, y_lo), mem: 4 (over y_hi, core).
Axes of the slice: x: 4, y: 4 (y_hi: 2, y_lo: 2; y = y_hi * 2 + y_lo), z: 8, core: 2. Of those that a mesh axis runs over, the one named last changes fastest.
Arguments:
- gradients: float32 [4, 16, 768, 3072], P('mem', None, 'lat', 'lon'), may hold values from -10 to 10
- ritz_vectors: float32 [80, 16, 256, 1024], P(None, 'mem', 'lat', 'lon'), may hold values from -6 to 6
- ritz_values: float32 [80], replicated, may hold values from 1.5 to 50
Outputs:
- preconditioned: float32 [4, 16, 768, 3072], P('mem', None, 'lat', 'lon')
- coefficients: float32 [4, 80], replicated
The draws below stay inside these ranges and needn't reach their ends.
All inputs are finite; a program needn't handle non-finite values.
Results may differ from the reference program's by a relative error of at most 0.00013.
Values sent between devices are 32-bit elements; how exact they have to be, the bound alone decides.
No kernel may reach another device: no remote copies, remote signals or barrier semaphores. Data moves between devices by JAX's collectives and lax.ppermute only.
A program may use at most 128 MiB of HBM per device.

```python
import math
import jax
import jax.numpy as jnp
from jax import lax

RITZ = 80
LEVELS = 16
MEMBERS = 4
COARSE_ROWS = 256
COARSE_COLS = 1024
FINE_ROWS = 768
FINE_COLS = 3072


def common_basis(key):
    values = jax.random.normal(key, (RITZ, LEVELS, COARSE_ROWS, COARSE_COLS), jnp.float32)
    return jnp.clip(values, -6.0, 6.0)


def draw_ritz_vectors(key, part):
    return common_basis(key)


def draw_gradients(key, part):
    vectors = common_basis(key)
    key = jax.random.fold_in(key, 11)
    amplitude_key, scatter_key = jax.random.split(key, 2)
    weights = jax.random.normal(amplitude_key, (MEMBERS, RITZ), jnp.float32)
    scatter_noise = jax.random.normal(scatter_key, (MEMBERS, LEVELS, FINE_ROWS, FINE_COLS), jnp.float32)
    pattern = jnp.einsum('mk,klyx->mlyx', weights, vectors, precision=lax.Precision.HIGHEST) * (1.0 / math.sqrt(RITZ))
    blocks = jnp.repeat(jnp.repeat(pattern, 3, axis=2), 3, axis=3)
    latitude_ramp = 0.5 + jnp.arange(FINE_ROWS, dtype=jnp.float32) * (1.0 / max(FINE_ROWS - 1, 1))
    values = latitude_ramp[None, None, :, None] * blocks + scatter_noise
    return jnp.clip(values, -10.0, 10.0)


def setup_inputs(seed: int = 0) -> dict:
    arg_keys = jax.random.split(jax.random.key(seed), 4)
    return {
        "gradients": draw_gradients(jax.random.fold_in(arg_keys[3], 71), 0),
        "ritz_vectors": draw_ritz_vectors(jax.random.fold_in(arg_keys[3], 71), 0),
        "ritz_values": jnp.clip(jnp.exp(jax.random.uniform(arg_keys[2], (RITZ,), jnp.float32, math.log(1.5), math.log(50.0))), 1.5, 50.0),
    }


TENT = (1.0 / 9.0, 2.0 / 9.0, 3.0 / 9.0, 2.0 / 9.0, 1.0 / 9.0)


def restrict_padded(padded):
    rows = (padded.shape[-2] - 2) // 3
    cols = (padded.shape[-1] - 2) // 3
    along = TENT[0] * padded[..., 0:3 * rows - 2:3, :]
    for offset in range(1, 5):
        along = along + TENT[offset] * padded[..., offset:offset + 3 * rows - 2:3, :]
    result = TENT[0] * along[..., 0:3 * cols - 2:3]
    for offset in range(1, 5):
        result = result + TENT[offset] * along[..., offset:offset + 3 * cols - 2:3]
    return result


def prolong_padded(padded):
    center = padded[..., 1:-1, :]
    first = (2.0 * center + padded[..., :-2, :]) * (1.0 / 3.0)
    third = (2.0 * center + padded[..., 2:, :]) * (1.0 / 3.0)
    stacked = jnp.stack([first, center, third], axis=-2)
    shape = stacked.shape
    rowwise = stacked.reshape(shape[:-3] + (shape[-3] * 3, shape[-1]))
    center = rowwise[..., 1:-1]
    first = (2.0 * center + rowwise[..., :-2]) * (1.0 / 3.0)
    third = (2.0 * center + rowwise[..., 2:]) * (1.0 / 3.0)
    stacked = jnp.stack([first, center, third], axis=-1)
    shape = stacked.shape
    return stacked.reshape(shape[:-2] + (shape[-2] * 3,))


def pad_grid(field):
    rank = field.ndim
    zeros_rows = [(0, 0)] * (rank - 2) + [(1, 1), (0, 0)]
    padded = jnp.pad(field, zeros_rows)
    wrap_cols = [(0, 0)] * (rank - 1) + [(1, 1)]
    return jnp.pad(padded, wrap_cols, mode="wrap")


def reference(gradients, ritz_vectors, ritz_values):
    coarse = lax.map(lambda member: restrict_padded(pad_grid(member)), gradients)
    scale = 1.0 / (LEVELS * COARSE_ROWS * COARSE_COLS)
    projections = jnp.einsum("klyx,mlyx->mk", ritz_vectors, coarse, precision=lax.Precision.HIGHEST) * scale
    coefficients = (1.0 / ritz_values - 1.0)[None, :] * projections
    corrected = coarse + jnp.einsum("klyx,mk->mlyx", ritz_vectors, coefficients, precision=lax.Precision.HIGHEST)
    preconditioned = lax.map(lambda member: prolong_padded(pad_grid(member)), corrected)
    return preconditioned, coefficients
```

```python
import jax
import jax.numpy as jnp
from jax import lax
from jax.experimental import pallas as pl
from jax.experimental.pallas import tpu as pltpu
from jax.sharding import PartitionSpec as P

F32 = jnp.float32
BF16 = jnp.bfloat16
RITZ = 80
GROUPS = 4
DEPTH = 4
ROWS = 32
COLS = 128
MAIN = DEPTH * ROWS
HALO = 16
BLOCK = MAIN + HALO
EDGE_ROWS = 16 * GROUPS
BAND = EDGE_ROWS + DEPTH * RITZ
SIDE = 2 * RITZ + 4 * GROUPS
CHUNK = 8
VMEM_LIMIT = 40 * 1024 * 1024


def iota(shape, dim):
    return lax.broadcasted_iota(jnp.int32, shape, dim)


def diagonal(rows):
    return iota((rows, COLS), 0) == iota((rows, COLS), 1)


def column_to_row(column, mask):
    spread = jnp.broadcast_to(column, mask.shape)
    return jnp.sum(jnp.where(mask, spread, 0.0), axis=0, keepdims=True)


def row_to_column(row, mask):
    spread = jnp.broadcast_to(row, mask.shape)
    return jnp.sum(jnp.where(mask, spread, 0.0), axis=1, keepdims=True)


def stack_rows(rows):
    position = iota((8, COLS), 0)
    result = jnp.zeros((8, COLS), F32)
    for index, row in enumerate(rows):
        result = jnp.where(position == index, jnp.broadcast_to(row, (8, COLS)), result)
    return result


def dot_split(value, weights):
    high = value.astype(BF16)
    low = (value - high.astype(F32)).astype(BF16)
    return jnp.dot(high, weights, preferred_element_type=F32) + jnp.dot(low, weights, preferred_element_type=F32)


def restrict_kernel(
    where_ref, g0_ref, g1_ref, g2_ref, first_ref, last_ref, x_ref, e_ref, h_ref, down_ref, up_ref, a_ref, w_ref
):
    step = pl.program_id(0)

    @pl.when(step == 0)
    def _():
        fine = iota((3 * COLS, 2 * COLS), 0)
        coarse = iota((3 * COLS, 2 * COLS), 1)
        tent = jnp.maximum(3 - jnp.abs(fine - 3 * coarse - 1), 0)
        left = jnp.logical_and(coarse == COLS, fine == 0)
        right = jnp.logical_and(coarse == COLS + 1, fine == 3 * COLS - 1)
        outer = jnp.where(jnp.logical_or(left, right), 1, 0)
        w_ref[...] = jnp.where(coarse < COLS, tent, outer).astype(F32).astype(BF16)

    position = iota((ROWS, COLS), 0)
    for part, g_ref in enumerate((g0_ref, g1_ref, g2_ref)):
        lanes = slice(COLS * part, COLS * (part + 1))
        for level in range(DEPTH):
            first = g_ref[0, level, pl.ds(0, ROWS, stride=3), :]
            middle = g_ref[0, level, pl.ds(1, ROWS, stride=3), :]
            third = g_ref[0, level, pl.ds(2, ROWS, stride=3), :]
            before = jnp.where(position == 0, 0.0, pltpu.roll(third, 1, 0))
            after = jnp.where(position == ROWS - 1, 0.0, pltpu.roll(first, ROWS - 1, 0))
            a_ref[ROWS * level : ROWS * (level + 1), lanes] = before + after + 2.0 * (first + third) + 3.0 * middle
            a_ref[MAIN + level : MAIN + level + 1, lanes] = first[0:1]
            a_ref[MAIN + DEPTH + level : MAIN + DEPTH + level + 1, lanes] = third[ROWS - 1 : ROWS]
    coarse = dot_split(a_ref[...], w_ref[...]) * (1.0 / 81.0)
    main, edge = coarse[:MAIN], coarse[MAIN:]
    e_ref[0] = main
    h_ref[0] = edge
    x_ref[0, :MAIN] = main[:, :COLS]
    x_ref[0, MAIN : MAIN + 8] = edge[:, :COLS]
    square, corner = diagonal(MAIN), diagonal(8)
    sides = []
    for lane in (COLS, COLS + 1):
        sides.append(column_to_row(main[:, lane : lane + 1], square))
        sides.append(column_to_row(edge[:, lane : lane + 1], corner))
    x_ref[0, MAIN + 8 : BLOCK] = stack_rows(sides)
    for ref, row, half in ((down_ref, ROWS - 1, edge[DEPTH:]), (up_ref, 0, edge[:DEPTH])):
        inner = [main[ROWS * level + row : ROWS * level + row + 1] for level in range(DEPTH)]
        sent = jnp.concatenate(inner + [half], axis=0)
        ref[pl.ds(16 * step, 8), :] = sent[:, :COLS]
        ref[pl.ds(16 * step + 8, 8), :] = sent[:, COLS:]
    down_ref[pl.ds(EDGE_ROWS + RITZ * step, RITZ), :] = last_ref[:, 0, 7, :]
    up_ref[pl.ds(EDGE_ROWS + RITZ * step, RITZ), :] = first_ref[:, 0, 0, :]


def sides_kernel(v_ref, above_ref, below_ref, e_ref, h_ref, left_ref, right_ref, e2_ref, h2_ref):
    step = pl.program_id(0)
    square, corner = diagonal(MAIN), diagonal(8)
    lanes = iota((CHUNK, COLS), 1)
    base = pl.multiple_of(step * CHUNK, CHUNK)
    for ref, lane in ((left_ref, 0), (right_ref, COLS - 1)):
        rows = []
        for k in range(CHUNK):
            vector = v_ref[k].reshape(MAIN, COLS)
            rows.append(column_to_row(vector[:, lane : lane + 1], square))
        ref[pl.ds(base, CHUNK), :] = stack_rows(rows)
        corners = jnp.zeros((CHUNK, COLS), F32)
        for index, source in ((0, above_ref), (DEPTH, below_ref)):
            for level in range(DEPTH):
                part = source[pl.ds(EDGE_ROWS + RITZ * level + base, CHUNK), :]
                spread = jnp.broadcast_to(part[:, lane : lane + 1], (CHUNK, COLS))
                corners = jnp.where(lanes == index + level, spread, corners)
        ref[pl.ds(RITZ + base, CHUNK), :] = corners

    @pl.when(step == 0)
    def _():
        position = iota((ROWS, 2 * COLS), 0)
        packed = ([], [])
        for group in range(GROUPS):
            start = 16 * group
            above = jnp.concatenate([above_ref[start : start + 8, :], above_ref[start + 8 : start + 16, :]], axis=1)
            below = jnp.concatenate([below_ref[start : start + 8, :], below_ref[start + 8 : start + 16, :]], axis=1)
            for level in range(DEPTH):
                rows = slice(ROWS * level, ROWS * (level + 1))
                tile = e_ref[group, rows, :]
                tile = tile + jnp.where(position == 0, above[DEPTH + level : DEPTH + level + 1, :], 0.0)
                tile = tile + jnp.where(position == ROWS - 1, below[DEPTH + level : DEPTH + level + 1, :], 0.0)
                e2_ref[group, rows, :] = tile
            edge = h_ref[group] + jnp.concatenate([above[:DEPTH], below[:DEPTH]], axis=0)
            h2_ref[group] = edge
            main = e2_ref[group]
            for rows, lane, outer in ((packed[0], 0, COLS), (packed[1], COLS - 1, COLS + 1)):
                for source in (lane, outer):
                    rows.append(column_to_row(main[:, source : source + 1], square))
                    rows.append(column_to_row(edge[:, source : source + 1], corner))
        for ref, rows in ((left_ref, packed[0]), (right_ref, packed[1])):
            ref[2 * RITZ : 2 * RITZ + 8, :] = stack_rows(rows[:8])
            ref[2 * RITZ + 8 : 2 * RITZ + 16, :] = stack_rows(rows[8:])


def edge_parts(above_ref, below_ref, left_ref, right_ref, start, count):
    parts = []
    for source in (above_ref, below_ref):
        for level in range(DEPTH):
            parts.append(source[pl.ds(EDGE_ROWS + RITZ * level + start, count), :])
    for source in (left_ref, right_ref):
        parts.append(source[pl.ds(start, count), :])
        parts.append(source[pl.ds(RITZ + start, count), :])
    return parts


def project_kernel(
    where_ref, v_ref, c0_ref, c1_ref, c2_ref, c3_ref, above_ref, below_ref, left_ref, right_ref, p_ref, s_ref
):
    step = pl.program_id(0)
    base = pl.multiple_of(step * CHUNK, CHUNK)
    blocks = (c0_ref, c1_ref, c2_ref, c3_ref)
    sums = [[jnp.zeros((8, COLS), F32) for _ in range(CHUNK)] for _ in blocks]
    for tile in range(MAIN // 8):
        level, row = divmod(8 * tile, ROWS)
        fields = [block[8 * tile : 8 * tile + 8, :] for block in blocks]
        for k in range(CHUNK):
            vector = v_ref[k, level, row : row + 8, :]
            for member in range(GROUPS):
                sums[member][k] = sums[member][k] + vector * fields[member]
    parts = edge_parts(above_ref, below_ref, left_ref, right_ref, base, CHUNK)
    for member in range(GROUPS):
        total = stack_rows([jnp.sum(value, axis=0, keepdims=True) for value in sums[member]])
        for index, part in enumerate(parts):
            total = total + part * blocks[member][MAIN + index : MAIN + index + 1, :]
        s_ref[member, pl.ds(base, CHUNK), :] = total

    @pl.when(step == pl.num_programs(0) - 1)
    def _():
        ones = jnp.ones((8, COLS), F32)
        for member in range(GROUPS):
            reduced = lax.dot_general(
                ones,
                s_ref[member],
                (((1,), (1,)), ((), ())),
                precision=lax.Precision.HIGHEST,
                preferred_element_type=F32,
            )
            p_ref[pl.ds(where_ref[0] ^ member, 1), :] = reduced[0:1, :]


def update_kernel(
    where_ref, c_ref, cv_ref, v_ref, above_ref, below_ref, left_ref, right_ref, u0_ref, u1_ref, u2_ref, u3_ref, t_ref
):
    step = pl.program_id(0)
    me = where_ref[0]
    outs = (u0_ref, u1_ref, u2_ref, u3_ref)

    def body(index, sums):
        sums = list(sums)
        for offset in range(CHUNK):
            k = index * CHUNK + offset
            weights = [c_ref[me ^ member, k] for member in range(GROUPS)]
            vector = v_ref[k, 0]
            for member in range(GROUPS):
                sums[member] = sums[member] + weights[member] * vector
        return tuple(sums)

    zeros = tuple(jnp.zeros((ROWS, COLS), F32) for _ in outs)
    sums = lax.fori_loop(0, RITZ // CHUNK, body, zeros)
    for member in range(GROUPS):
        outs[member][pl.ds(pl.multiple_of(step * ROWS, ROWS), ROWS), :] = sums[member]

    @pl.when(step == 0)
    def _():
        parts = edge_parts(above_ref, below_ref, left_ref, right_ref, 0, RITZ)
        for index, part in enumerate(parts):
            t_ref[index] = jnp.dot(
                cv_ref[...], part, precision=lax.Precision.HIGHEST, preferred_element_type=F32
            )
        for member in range(GROUPS):
            for index in range(len(parts)):
                outs[member][MAIN + index : MAIN + index + 1, :] = t_ref[index, pl.ds(me ^ member, 1), :]
            outs[member][MAIN + 12 : BLOCK, :] = jnp.zeros((4, COLS), F32)


def prolong_kernel(
    where_ref, r0_ref, r1_ref, r2_ref, r3_ref, e2_ref, h2_ref, left_ref, right_ref, o_ref, r_ref, a_ref, f_ref, z_ref, m_ref
):
    step = pl.program_id(0)

    @pl.when(step == 0)
    def _():
        coarse = iota((2 * COLS, 3 * COLS), 0)
        fine = iota((2 * COLS, 3 * COLS), 1)
        tent = jnp.maximum(3 - jnp.abs(fine - 3 * coarse - 1), 0)
        left = jnp.logical_and(coarse == COLS, fine == 0)
        right = jnp.logical_and(coarse == COLS + 1, fine == 3 * COLS - 1)
        outer = jnp.where(jnp.logical_or(left, right), 1, 0)
        z_ref[...] = jnp.where(coarse < COLS, tent, outer).astype(F32).astype(BF16)

    for member, ref in enumerate((r0_ref, r1_ref, r2_ref, r3_ref)):

        @pl.when(step == member)
        def _(ref=ref):
            r_ref[...] = ref[...]

    square, corner = diagonal(MAIN), diagonal(8)
    start = 2 * RITZ + 4 * step
    halves = []
    for index, (rows, mask, edge) in enumerate(((MAIN, square, e2_ref), (8, corner, h2_ref))):
        offset = MAIN * index
        lanes = iota((rows, COLS), 1)
        value = edge[0, :, :COLS] + r_ref[offset : offset + rows, :]
        outer = edge[0, :, COLS:]
        for slot, (ref, lane) in enumerate(((left_ref, 0), (right_ref, COLS - 1))):
            beyond = ref[pl.ds(start + index, 1), :] + r_ref[MAIN + 8 + 2 * slot + index : MAIN + 9 + 2 * slot + index, :]
            inner = ref[pl.ds(start + 2 + index, 1), :]
            outer = outer + jnp.where(lanes == slot, row_to_column(beyond, mask), 0.0)
            value = value + jnp.where(lanes == lane, row_to_column(inner, mask), 0.0)
        halves.append((value, outer))
    a_ref[:MAIN, :COLS] = halves[0][0]
    a_ref[:MAIN, COLS:] = halves[0][1]
    position = iota((8, COLS), 0)
    keep_above = jnp.where(position < DEPTH, where_ref[1], where_ref[2]).astype(F32)
    a_ref[MAIN:, :COLS] = halves[1][0] * keep_above
    a_ref[MAIN:, COLS:] = halves[1][1] * keep_above
    f_ref[...] = dot_split(a_ref[...], z_ref[...])
    position = iota((ROWS, 3 * COLS), 0)
    for level in range(DEPTH):
        center = f_ref[ROWS * level : ROWS * (level + 1), :]
        above = f_ref[MAIN + level : MAIN + level + 1, :]
        below = f_ref[MAIN + DEPTH + level : MAIN + DEPTH + level + 1, :]
        before = jnp.where(position == 0, above, pltpu.roll(center, 1, 0))
        after = jnp.where(position == ROWS - 1, below, pltpu.roll(center, ROWS - 1, 0))
        fine = ((2.0 * center + before) * (1.0 / 9.0), center * (1.0 / 3.0), (2.0 * center + after) * (1.0 / 9.0))
        for part in range(3):
            lanes = slice(COLS * part, COLS * (part + 1))
            for offset, value in enumerate(fine):
                m_ref[level, part, pl.ds(offset, ROWS, stride=3), :] = value[:, lanes]
            o_ref[0, level, :, lanes] = m_ref[level, part]


def whole(shape):
    return pl.BlockSpec(shape, lambda i, *_: (0,) * len(shape))


def struct(*shape):
    return jax.ShapeDtypeStruct(shape, F32)


def params():
    return pltpu.CompilerParams(vmem_limit_bytes=VMEM_LIMIT)


def restrict(place, gradients, ritz_vectors):
    return pl.pallas_call(
        restrict_kernel,
        grid_spec=pltpu.PrefetchScalarGridSpec(
            num_scalar_prefetch=1,
            grid=(GROUPS,),
            in_specs=[
                pl.BlockSpec((1, DEPTH, 3 * ROWS, COLS), lambda i, place: (0, i ^ place[0], 0, 0)),
                pl.BlockSpec((1, DEPTH, 3 * ROWS, COLS), lambda i, place: (0, i ^ place[0], 0, 1)),
                pl.BlockSpec((1, DEPTH, 3 * ROWS, COLS), lambda i, place: (0, i ^ place[0], 0, 2)),
                pl.BlockSpec((RITZ, 1, 8, COLS), lambda i, place: (0, i, 0, 0)),
                pl.BlockSpec((RITZ, 1, 8, COLS), lambda i, place: (0, i, ROWS // 8 - 1, 0)),
            ],
            out_specs=[
                pl.BlockSpec((1, BLOCK, COLS), lambda i, place: (i, 0, 0)),
                pl.BlockSpec((1, MAIN, 2 * COLS), lambda i, place: (i, 0, 0)),
                pl.BlockSpec((1, 8, 2 * COLS), lambda i, place: (i, 0, 0)),
                whole((BAND, COLS)),
                whole((BAND, COLS)),
            ],
            scratch_shapes=[
                pltpu.VMEM((MAIN + 8, 3 * COLS), F32),
                pltpu.VMEM((3 * COLS, 2 * COLS), BF16),
            ],
        ),
        out_shape=[
            struct(GROUPS, BLOCK, COLS),
            struct(GROUPS, MAIN, 2 * COLS),
            struct(GROUPS, 8, 2 * COLS),
            struct(BAND, COLS),
            struct(BAND, COLS),
        ],
        compiler_params=params(),
        name="restrict",
    )(place, gradients, gradients, gradients, ritz_vectors, ritz_vectors)


def sides(ritz_vectors, above, below, main, edge):
    return pl.pallas_call(
        sides_kernel,
        grid=(RITZ // CHUNK,),
        in_specs=[
            pl.BlockSpec((CHUNK, DEPTH, ROWS, COLS), lambda i: (i, 0, 0, 0)),
            whole((BAND, COLS)),
            whole((BAND, COLS)),
            whole((GROUPS, MAIN, 2 * COLS)),
            whole((GROUPS, 8, 2 * COLS)),
        ],
        out_specs=[
            whole((SIDE, COLS)),
            whole((SIDE, COLS)),
            whole((GROUPS, MAIN, 2 * COLS)),
            whole((GROUPS, 8, 2 * COLS)),
        ],
        out_shape=[
            struct(SIDE, COLS),
            struct(SIDE, COLS),
            struct(GROUPS, MAIN, 2 * COLS),
            struct(GROUPS, 8, 2 * COLS),
        ],
        compiler_params=params(),
        name="sides",
    )(ritz_vectors, above, below, main, edge)


def project(place, ritz_vectors, blocks, messages):
    return pl.pallas_call(
        project_kernel,
        grid_spec=pltpu.PrefetchScalarGridSpec(
            num_scalar_prefetch=1,
            grid=(RITZ // CHUNK,),
            in_specs=[pl.BlockSpec((CHUNK, DEPTH, ROWS, COLS), lambda i, place: (i, 0, 0, 0))]
            + [whole((BLOCK, COLS))] * 4
            + [whole((BAND, COLS))] * 2
            + [whole((SIDE, COLS))] * 2,
            out_specs=whole((GROUPS, RITZ)),
            scratch_shapes=[pltpu.VMEM((GROUPS, RITZ, COLS), F32)],
        ),
        out_shape=struct(GROUPS, RITZ),
        compiler_params=params(),
        name="project",
    )(place, ritz_vectors, *blocks, *messages)


def update(place, coefficients, ritz_vectors, messages):
    return pl.pallas_call(
        update_kernel,
        grid_spec=pltpu.PrefetchScalarGridSpec(
            num_scalar_prefetch=1,
            grid=(DEPTH,),
            in_specs=[
                pl.BlockSpec(memory_space=pltpu.SMEM),
                whole((8, RITZ)),
                pl.BlockSpec((RITZ, 1, ROWS, COLS), lambda i, place: (0, i, 0, 0)),
            ]
            + [whole((BAND, COLS))] * 2
            + [whole((SIDE, COLS))] * 2,
            out_specs=[whole((BLOCK, COLS))] * 4,
            scratch_shapes=[pltpu.VMEM((12, 8, COLS), F32)],
        ),
        out_shape=[struct(BLOCK, COLS)] * 4,
        compiler_params=params(),
        name="update",
    )(place, coefficients, jnp.concatenate([coefficients, coefficients], axis=0), ritz_vectors, *messages)


def prolong(place, returned, main, edge, left, right):
    return pl.pallas_call(
        prolong_kernel,
        grid_spec=pltpu.PrefetchScalarGridSpec(
            num_scalar_prefetch=1,
            grid=(GROUPS,),
            in_specs=[whole((BLOCK, COLS))] * 4
            + [
                pl.BlockSpec((1, MAIN, 2 * COLS), lambda i, place: (i, 0, 0)),
                pl.BlockSpec((1, 8, 2 * COLS), lambda i, place: (i, 0, 0)),
                whole((SIDE, COLS)),
                whole((SIDE, COLS)),
            ],
            out_specs=pl.BlockSpec((1, DEPTH, 3 * ROWS, 3 * COLS), lambda i, place: (0, i ^ place[0], 0, 0)),
            scratch_shapes=[
                pltpu.VMEM((BLOCK, COLS), F32),
                pltpu.VMEM((MAIN + 8, 2 * COLS), F32),
                pltpu.VMEM((MAIN + 8, 3 * COLS), F32),
                pltpu.VMEM((2 * COLS, 3 * COLS), BF16),
                pltpu.VMEM((DEPTH, 3, 3 * ROWS, COLS), F32),
            ],
        ),
        out_shape=struct(1, GROUPS * DEPTH, 3 * ROWS, 3 * COLS),
        compiler_params=params(),
        name="prolong",
    )(place, *returned, main, edge, left, right)


def exchange_members(blocks):
    size = lax.axis_size("mem")
    return [blocks[0]] + [
        lax.ppermute(blocks[shift], "mem", [(i, i ^ shift) for i in range(size)]) for shift in range(1, size)
    ]


def exchange_sum(value, axes):
    size = lax.axis_size(axes)
    copies = jnp.broadcast_to(value[None], (size,) + value.shape)
    return jnp.sum(lax.all_to_all(copies, axes, 0, 0, tiled=True), axis=0)


def per_device(gradients, ritz_vectors, ritz_values):
    lats, lons = lax.axis_size("lat"), lax.axis_size("lon")
    lat, mem = lax.axis_index("lat"), lax.axis_index("mem")
    place = jnp.stack([mem, jnp.where(lat > 0, 1, 0), jnp.where(lat < lats - 1, 1, 0)]).astype(jnp.int32)

    blocks, main, edge, down, up = restrict(place, gradients, ritz_vectors)
    above = lax.ppermute(down, "lat", [(i, i + 1) for i in range(lats - 1)])
    below = lax.ppermute(up, "lat", [(i + 1, i) for i in range(lats - 1)])
    spread = exchange_members([blocks[i] for i in range(GROUPS)])
    to_left, to_right, main, edge = sides(ritz_vectors, above, below, main, edge)
    right = lax.ppermute(to_left, "lon", [((i + 1) % lons, i) for i in range(lons)])
    left = lax.ppermute(to_right, "lon", [(i, (i + 1) % lons) for i in range(lons)])
    messages = (above, below, left, right)

    partial = project(place, ritz_vectors, spread, messages)
    projections = exchange_sum(exchange_sum(partial, ("lon", "mem")), "lat")
    cells = GROUPS * DEPTH * ROWS * lats * COLS * lons
    coefficients = (1.0 / ritz_values - 1.0)[None, :] * (projections * (1.0 / cells))

    returned = exchange_members(update(place, coefficients, ritz_vectors, messages))
    preconditioned = prolong(place, returned, main, edge, left, right)
    return preconditioned, coefficients


def solution(mesh):
    placed = (P("mem", None, "lat", "lon"), P(None, "mem", "lat", "lon"), P())
    return jax.shard_map(
        per_device,
        mesh=mesh,
        in_specs=placed,
        out_specs=(P("mem", None, "lat", "lon"), P()),
        check_vma=False,
    )
```

```python
import functools

import jax
import jax.numpy as jnp
from jax import lax
from jax.experimental import pallas as pl
from jax.experimental.pallas import tpu as pltpu
from jax.sharding import PartitionSpec as P

F32 = jnp.float32
BF16 = jnp.bfloat16
RITZ = 80
GROUPS = 4
DEPTH = 4
ROWS = 32
COLS = 128
MAIN = DEPTH * ROWS
HALO = 16
BLOCK = MAIN + HALO
LEVELS = GROUPS * DEPTH
BAND = 2 * 3 * LEVELS
EDGE = DEPTH * RITZ
SIDE = RITZ + 4 * GROUPS
CHUNK = 8
PIECES = 4
EARLY = (0, 2)
LATE = (3, 1)
MIB = 1024 * 1024
VMEM_LIMIT = 24 * MIB


def iota(shape, dim):
    return lax.broadcasted_iota(jnp.int32, shape, dim)


def diagonal(rows):
    return iota((rows, COLS), 0) == iota((rows, COLS), 1)


def column_to_row(column, mask):
    spread = jnp.broadcast_to(column, mask.shape)
    return jnp.sum(jnp.where(mask, spread, 0.0), axis=0, keepdims=True)


def stack_rows(rows):
    position = iota((8, COLS), 0)
    result = jnp.zeros((8, COLS), F32)
    for index, row in enumerate(rows):
        result = jnp.where(position == index, jnp.broadcast_to(row, (8, COLS)), result)
    return result


def split(value):
    high = value.astype(BF16)
    return high, (value - high.astype(F32)).astype(BF16)


def dot_split(value, weights):
    rows = value.shape[0]
    both = jnp.dot(jnp.concatenate(split(value), axis=0), weights, preferred_element_type=F32)
    return both[:rows] + both[rows:]


def tent_weights(coarse, fine):
    tent = jnp.maximum(3 - jnp.abs(fine - 3 * coarse - 1), 0)
    left = jnp.logical_and(coarse == COLS, fine == 0)
    right = jnp.logical_and(coarse == COLS + 1, fine == 3 * COLS - 1)
    outer = jnp.where(jnp.logical_or(left, right), 1, 0)
    return jnp.where(coarse < COLS, tent, outer)


def edges_kernel(g_ref, f_ref, down_ref, up_ref, sem):
    copies = []
    for part in range(3):
        source = g_ref.at[:, :, pl.ds(COLS * part, COLS)]
        copy = pltpu.make_async_copy(source, f_ref.at[part], sem.at[part])
        copy.start()
        copies.append(copy)
    row = iota((1, 8, COLS), 1)
    plans = (
        (up_ref, 0, jnp.where(row < 4, jnp.where(row == 1, 3, jnp.where(row == 3, 1, 2)), 0), row == 0),
        (
            down_ref,
            3 * ROWS - 8,
            jnp.where(row > 3, jnp.where(row == 6, 3, jnp.where(row == 4, 1, 2)), 0),
            row == 7,
        ),
    )
    for part in range(3):
        copies[part].wait()
        for ref, start, weights, outer in plans:
            fine = f_ref[part, :, start : start + 8, :]
            place = 2 * LEVELS * part
            ref[place : place + LEVELS, :] = jnp.sum(fine * weights.astype(F32), axis=1)
            ref[place + LEVELS : place + 2 * LEVELS, :] = jnp.sum(jnp.where(outer, fine, 0.0), axis=1)


def restrict_kernel(f_ref, v_ref, copy_ref, e_ref, h_ref, first_ref, last_ref, w_ref, a_ref, o_ref, m_ref, sem):
    rows = RITZ * MAIN // PIECES
    copies = []
    for piece in range(PIECES):
        place = pl.ds(rows * piece, rows)
        copy = pltpu.make_async_copy(v_ref.at[place, :], copy_ref.at[place, :], sem.at[piece])
        copy.start()
        copies.append(copy)
    fine = iota((3 * COLS, 2 * COLS), 0)
    coarse = iota((3 * COLS, 2 * COLS), 1)
    w_ref[...] = tent_weights(coarse, fine).astype(F32).astype(BF16)
    position = iota((ROWS, COLS), 0)
    o_ref[...] = jnp.zeros_like(o_ref)

    def body(group, carry):
        for part in range(3):
            lanes = slice(COLS * part, COLS * (part + 1))
            for level in range(DEPTH):
                first = f_ref[part, DEPTH * group + level, pl.ds(0, ROWS, stride=3), :]
                middle = f_ref[part, DEPTH * group + level, pl.ds(1, ROWS, stride=3), :]
                third = f_ref[part, DEPTH * group + level, pl.ds(2, ROWS, stride=3), :]
                before = jnp.where(position == 0, 0.0, pltpu.roll(third, 1, 0))
                after = jnp.where(position == ROWS - 1, 0.0, pltpu.roll(first, ROWS - 1, 0))
                high, low = split(before + after + 2.0 * (first + third) + 3.0 * middle)
                start = ROWS * level
                a_ref[start : start + ROWS, lanes] = high
                a_ref[BLOCK + start : BLOCK + start + ROWS, lanes] = low
                o_ref[level : level + 1, lanes] = first[0:1]
                o_ref[DEPTH + level : DEPTH + level + 1, lanes] = third[ROWS - 1 : ROWS]
        high, low = split(o_ref[...])
        a_ref[MAIN:BLOCK, :] = high
        a_ref[BLOCK + MAIN :, :] = low
        both = jnp.dot(a_ref[...], w_ref[...], preferred_element_type=F32)
        coarse = (both[:BLOCK] + both[BLOCK:]) * (1.0 / 81.0)
        e_ref[group] = coarse[:MAIN]
        h_ref[group] = coarse[MAIN : MAIN + 8]
        return carry

    lax.fori_loop(0, GROUPS, body, 0)
    lanes = iota((MAIN, COLS), 1) // 2
    half = RITZ // 2
    for part in range(2):
        packed = jnp.zeros((MAIN, COLS), F32)
        for index in range(half):
            k = half * part + index
            if k % (RITZ // PIECES) == 0:
                copies[k // (RITZ // PIECES)].wait()
            turned = pltpu.roll(copy_ref[MAIN * k : MAIN * (k + 1), :], 2 * index + 1, 1)
            packed = jnp.where(lanes == index, turned, packed)
        m_ref[...] = jnp.transpose(packed)
        place = slice(half * part, half * (part + 1))
        last_ref[place, :] = m_ref[pl.ds(0, half, stride=2), :]
        first_ref[place, :] = m_ref[pl.ds(1, half, stride=2), :]


def sides_kernel(
    where_ref, above_ref, below_ref, e_ref, h_ref, first_ref, last_ref, w_ref,
    left_ref, right_ref, e2_ref, h2_ref, x0_ref, x1_ref, x2_ref, x3_ref, m_ref
):
    corner = diagonal(8)
    left_ref[:RITZ, :] = first_ref[...]
    right_ref[:RITZ, :] = last_ref[...]
    position = iota((ROWS, 2 * COLS), 0)
    lanes = iota((MAIN, COLS), 1)
    packed = jnp.zeros((MAIN, COLS), F32)
    corners = ([], [])
    received = []
    for index, ref in enumerate((above_ref, below_ref)):
        keep = where_ref[1 + index].astype(F32)
        parts = [keep * ref[2 * LEVELS * part : 2 * LEVELS * (part + 1), :] for part in range(3)]
        received.append(jnp.concatenate(parts, axis=1))
    received = dot_split(jnp.concatenate(received, axis=0), w_ref[...]) * (1.0 / 81.0)
    for group in range(GROUPS):
        place = slice(DEPTH * group, DEPTH * (group + 1))
        over, above, under, below = [received[LEVELS * i : LEVELS * (i + 1)][place] for i in range(4)]
        for level in range(DEPTH):
            rows = slice(ROWS * level, ROWS * (level + 1))
            tile = e_ref[group, rows, :]
            tile = tile + jnp.where(position == 0, above[level : level + 1, :], 0.0)
            tile = tile + jnp.where(position == ROWS - 1, below[level : level + 1, :], 0.0)
            e2_ref[group, rows, :] = tile
        edge = h_ref[group] + jnp.concatenate([over, under], axis=0)
        h2_ref[group] = edge
        for rows, lane, outer in ((corners[0], 0, COLS), (corners[1], COLS - 1, COLS + 1)):
            for source in (lane, outer):
                rows.append(column_to_row(edge[:, source : source + 1], corner))
        inner = pltpu.roll(e2_ref[group, :, :COLS], 4 * group + 1, 1)
        outer = pltpu.roll(e2_ref[group, :, COLS:], 4 * group + 2, 1)
        packed = jnp.where(lanes // 2 == 2 * group, inner, packed)
        packed = jnp.where(lanes // 2 == 2 * group + 1, outer, packed)
    m_ref[...] = jnp.transpose(packed)
    for ref, row, outer, extra in ((left_ref, 1, 2, corners[0]), (right_ref, 0, 3, corners[1])):
        for pair in range(2):
            rows = []
            for group in (2 * pair, 2 * pair + 1):
                rows.append(m_ref[4 * group + row : 4 * group + row + 1, :])
                rows.append(extra[2 * group])
                rows.append(m_ref[4 * group + outer : 4 * group + outer + 1, :])
                rows.append(extra[2 * group + 1])
            ref[RITZ + 8 * pair : RITZ + 8 * pair + 8, :] = stack_rows(rows)
    for slot, ref in enumerate((x0_ref, x1_ref, x2_ref, x3_ref)):
        group = where_ref[0] ^ slot
        ref[:MAIN] = e2_ref[group, :, :COLS]
        ref[MAIN:] = stack_rows([m_ref[pl.ds(4 * group + 2 + side, 1), :] for side in range(2)])


def bands_kernel(v_ref, left_ref, right_ref, down_ref, up_ref):
    lanes = iota((RITZ, COLS), 1)
    for ref, row in ((up_ref, 0), (down_ref, ROWS - 1)):
        corners = jnp.zeros((RITZ, COLS), F32)
        for level in range(DEPTH):
            source = ROWS * level + row
            ref[RITZ * level : RITZ * (level + 1), :] = v_ref[pl.ds(source, RITZ, stride=MAIN), :]
            for side, columns in enumerate((left_ref, right_ref)):
                target = DEPTH * side + level
                turned = pltpu.roll(columns[:RITZ, :], (target - source) % COLS, 1)
                corners = jnp.where(lanes == target, turned, corners)
        ref[EDGE:, :] = corners


def edge_parts(where_ref, above_ref, below_ref, left_ref, right_ref):
    keep = [where_ref[1 + index].astype(F32) for index in range(2)]
    parts = []
    for index, source in enumerate((above_ref, below_ref)):
        for level in range(DEPTH):
            parts.append(keep[index] * source[RITZ * level : RITZ * (level + 1), :])
    parts += [left_ref[:RITZ, :], keep[0] * above_ref[EDGE:, :], right_ref[:RITZ, :], keep[1] * below_ref[EDGE:, :]]
    return parts


def accumulate(v_ref, blocks, base):
    sums = [[jnp.zeros((8, COLS), F32) for _ in range(CHUNK)] for _ in blocks]
    for tile in range(MAIN // 8):
        fields = [block[8 * tile : 8 * tile + 8, :] for block in blocks]
        for k in range(CHUNK):
            vector = v_ref[pl.ds(pl.multiple_of((base + k) * MAIN + 8 * tile, 8), 8), :]
            for member, field in enumerate(fields):
                sums[member][k] = sums[member][k] + vector * field
    return [stack_rows([jnp.sum(value, axis=0, keepdims=True) for value in member]) for member in sums]


def near_kernel(v_ref, c0_ref, c2_ref, s_ref):
    def body(step, carry):
        base = pl.multiple_of(step * CHUNK, CHUNK)
        for member, total in enumerate(accumulate(v_ref, (c0_ref, c2_ref), base)):
            s_ref[member, pl.ds(base, CHUNK), :] = total
        return carry

    lax.fori_loop(0, RITZ // CHUNK, body, 0)


def far_kernel(
    where_ref, near_ref, v_ref, c0_ref, c1_ref, c2_ref, c3_ref, left_ref, right_ref, p_ref, s_ref
):
    blocks = (c0_ref, c2_ref, c3_ref, c1_ref)

    def body(step, carry):
        base = pl.multiple_of(step * CHUNK, CHUNK)
        totals = [near_ref[member, pl.ds(base, CHUNK), :] for member in range(2)]
        totals += accumulate(v_ref, (c3_ref, c1_ref), base)
        parts = [ref[pl.ds(base, CHUNK), :] for ref in (left_ref, right_ref)]
        for member, total in enumerate(totals):
            for index, part in enumerate(parts):
                total = total + part * blocks[member][MAIN + index : MAIN + index + 1, :]
            s_ref[member, pl.ds(base, CHUNK), :] = total
        return carry

    lax.fori_loop(0, RITZ // CHUNK, body, 0)
    ones = jnp.ones((8, COLS), F32)
    for index, slot in enumerate((0, 2, 3, 1)):
        reduced = exact_dot(ones, s_ref[index], ((1,), (1,)))
        p_ref[pl.ds(where_ref[0] ^ slot, 1), :] = reduced[0:1, :]


def exact_dot(left, right, dims):
    return lax.dot_general(
        left, right, (dims, ((), ())), precision=lax.Precision.HIGHEST, preferred_element_type=F32
    )


def weighted_sums(v_ref, b_ref, slots, prepare):
    half = MAIN // 2
    results = []
    for part in range(2):

        def body(index, sums, part=part):
            sums = list(sums)
            prepare(part, index)
            for offset in range(CHUNK):
                k = index * CHUNK + offset
                vector = v_ref[k, part]
                for position, member in enumerate(slots):
                    sums[position] = sums[position] + b_ref[pl.ds(RITZ * member + k, 1), :] * vector
            return tuple(sums)

        zeros = tuple(jnp.zeros((half, COLS), F32) for _ in slots)
        results.append(lax.fori_loop(0, RITZ // CHUNK, body, zeros))
    return results


def update_kernel(
    where_ref, c_ref, v_hbm_ref, above_ref, below_ref, left_ref, right_ref,
    v_ref, b_ref, edge_ref, u1_ref, u2_ref, u3_ref, sem
):
    me = where_ref[0]
    outs = (None, u1_ref, u2_ref, u3_ref)
    pieces = RITZ // CHUNK

    def copy(part, piece):
        place = pl.ds(piece * CHUNK, CHUNK)
        return pltpu.make_async_copy(v_hbm_ref.at[place, part], v_ref.at[place, part], sem.at[part, piece])

    for part in range(2):
        for piece in range(pieces):
            copy(part, piece).start()
    coefficients = c_ref[...]
    for member in range(GROUPS):
        chosen = jnp.where(iota((8, COLS), 0) == (me ^ member), 1.0, 0.0)
        b_ref[RITZ * member : RITZ * (member + 1), :] = exact_dot(coefficients, chosen, ((0,), (0,)))
    swap = jnp.where(iota((8, 8), 1) == (me ^ iota((8, 8), 0)), 1.0, 0.0)
    ordered = exact_dot(swap, coefficients, ((1,), (0,)))
    parts = edge_parts(where_ref, above_ref, below_ref, left_ref, right_ref)
    edge = exact_dot(ordered, jnp.concatenate(parts, axis=1), ((1,), (0,)))
    for member in range(GROUPS):
        ref, start = (outs[member], MAIN) if member else (edge_ref, 0)
        for index in range(len(parts)):
            row = edge[member : member + 1, COLS * index : COLS * (index + 1)]
            ref[start + index : start + index + 1, :] = row
        ref[start + 12 : start + HALO, :] = jnp.zeros((4, COLS), F32)

    def prepare(part, index):
        copy(part, index).wait()

    half = MAIN // 2
    for part, sums in enumerate(weighted_sums(v_ref, b_ref, (1, 2, 3), prepare)):
        for member, value in zip((1, 2, 3), sums):
            outs[member][half * part : half * (part + 1), :] = value


def own_kernel(v_ref, b_ref, edge_ref, u0_ref):
    half = MAIN // 2
    for part, sums in enumerate(weighted_sums(v_ref, b_ref, (0,), lambda part, index: None)):
        u0_ref[half * part : half * (part + 1), :] = sums[0]
    u0_ref[MAIN:, :] = edge_ref[...]


def write_group(o_ref, m_ref, group, index, sem):
    copies = []
    for part in range(3):
        target = o_ref.at[pl.ds(DEPTH * group, DEPTH), :, pl.ds(COLS * part, COLS)]
        copy = pltpu.make_async_copy(m_ref.at[index, part], target, sem.at[index, part])
        copy.start()
        copies.append(copy)
    return copies


def prolong_kernel(slots, where_ref, ra_ref, rb_ref, e2_ref, h2_ref, left_ref, right_ref, *refs):
    early_ref = None
    copies = []
    if len(refs) == 4:
        m_ref, a_ref, f_ref, z_ref = refs
    else:
        early_ref, o_ref, a_ref, f_ref, z_ref, m_ref, early_sem, sem = refs
        for index, slot in enumerate(EARLY):
            copies += write_group(o_ref, early_ref, where_ref[0] ^ slot, index, early_sem)
    coarse = iota((2 * COLS, 3 * COLS), 0)
    fine = iota((2 * COLS, 3 * COLS), 1)
    coarse = jnp.where(coarse == COLS + 2, 0, jnp.where(coarse == COLS + 3, COLS - 1, coarse))
    z_ref[...] = tent_weights(coarse, fine).astype(F32).astype(BF16)
    row = iota((8, COLS), 0)
    keep = jnp.where(row < DEPTH, where_ref[1], where_ref[2]).astype(F32)
    outer_lanes = iota((MAIN, COLS), 1) < 4
    position = iota((ROWS, 3 * COLS), 0)
    for index, (slot, r_ref) in enumerate(zip(slots, (ra_ref, rb_ref))):
        group = where_ref[0] ^ slot
        start = RITZ + 4 * group
        outer = [r_ref[MAIN + 8 + kind : MAIN + 9 + kind, :] for kind in range(4)]
        first_half = iota((1, COLS), 1) < DEPTH
        beyond = (
            (outer[0], outer[2]),
            (
                jnp.where(first_half, outer[1], pltpu.roll(outer[3], DEPTH, 1)),
                jnp.where(first_half, pltpu.roll(outer[1], COLS - DEPTH, 1), outer[3]),
            ),
        )
        rows = []
        for kind in range(2):
            for ref, value in zip((left_ref, right_ref), beyond[kind]):
                rows.append(ref[pl.ds(start + kind, 1), :] + value)
            for ref in (left_ref, right_ref):
                rows.append(ref[pl.ds(start + 2 + kind, 1), :])
        stacked = jnp.concatenate([stack_rows(rows), jnp.zeros((COLS - 8, COLS), F32)], axis=0)
        turned = jnp.transpose(stacked)
        corners = pltpu.roll(turned[:8], COLS - 4, 1)
        a_ref[:MAIN, :COLS] = e2_ref[group, :, :COLS] + r_ref[:MAIN, :]
        a_ref[:MAIN, COLS:] = e2_ref[group, :, COLS:] + jnp.where(outer_lanes, turned, 0.0)
        a_ref[MAIN:, :COLS] = (h2_ref[group, :, :COLS] + r_ref[MAIN : MAIN + 8, :]) * keep
        a_ref[MAIN:, COLS:] = (h2_ref[group, :, COLS:] + jnp.where(outer_lanes[:8], corners, 0.0)) * keep
        f_ref[...] = dot_split(a_ref[...], z_ref[...])
        for level in range(DEPTH):
            center = f_ref[ROWS * level : ROWS * (level + 1), :]
            above = f_ref[MAIN + level : MAIN + level + 1, :]
            below = f_ref[MAIN + DEPTH + level : MAIN + DEPTH + level + 1, :]
            before = jnp.where(position == 0, above, pltpu.roll(center, 1, 0))
            after = jnp.where(position == ROWS - 1, below, pltpu.roll(center, ROWS - 1, 0))
            fine = ((2.0 * center + before) * (1.0 / 9.0), center * (1.0 / 3.0), (2.0 * center + after) * (1.0 / 9.0))
            for part in range(3):
                lanes = slice(COLS * part, COLS * (part + 1))
                for offset, value in enumerate(fine):
                    m_ref[index, part, level, pl.ds(offset, ROWS, stride=3), :] = value[:, lanes]
        if early_ref is not None:
            copies += write_group(o_ref, m_ref, group, index, sem)
    for copy in copies:
        copy.wait()


def struct(*shape):
    return jax.ShapeDtypeStruct(shape, F32)


SMEM = pl.BlockSpec(memory_space=pltpu.SMEM)
VMEM = pl.BlockSpec(memory_space=pltpu.VMEM)
HBM = pl.BlockSpec(memory_space=pltpu.HBM)
FIELD = (GROUPS, MAIN, 2 * COLS)
RIM = (GROUPS, 8, 2 * COLS)


def call(kernel, name, ins, outs, scratch, out_specs=None, limit=VMEM_LIMIT, aliases=None):
    return pl.pallas_call(
        kernel,
        in_specs=ins,
        out_specs=out_specs or [VMEM] * len(outs),
        out_shape=outs,
        scratch_shapes=scratch,
        input_output_aliases=aliases or {},
        compiler_params=pltpu.CompilerParams(vmem_limit_bytes=limit),
        name=name,
    )


def edges(gradients):
    scratch = [pltpu.SemaphoreType.DMA((3,))]
    outs = [pltpu.VMEM((3, LEVELS, 3 * ROWS, COLS), F32)] + [struct(BAND, COLS)] * 2
    gradients = pltpu.with_memory_space_constraint(gradients, pltpu.HBM)
    return call(edges_kernel, "edges", [HBM], outs, scratch, limit=VMEM_LIMIT)(gradients)


def restrict(fine, ritz_vectors):
    scratch = [
        pltpu.VMEM((2 * BLOCK, 3 * COLS), BF16),
        pltpu.VMEM((HALO, 3 * COLS), F32),
        pltpu.VMEM((COLS, COLS), F32),
        pltpu.SemaphoreType.DMA((PIECES,)),
    ]
    outs = [pltpu.VMEM((RITZ * MAIN, COLS), F32), struct(*FIELD), struct(*RIM)] + [struct(RITZ, COLS)] * 2
    outs += [jax.ShapeDtypeStruct((3 * COLS, 2 * COLS), BF16)]
    flat = ritz_vectors.reshape(RITZ * MAIN, COLS)
    flat = pltpu.with_memory_space_constraint(flat, pltpu.HBM)
    return call(restrict_kernel, "restrict", [VMEM, HBM], outs, scratch, limit=VMEM_LIMIT)(fine, flat)


def sides(*args):
    outs = [struct(SIDE, COLS)] * 2 + [struct(*FIELD), struct(*RIM)] + [struct(MAIN + 8, COLS)] * 4
    return call(sides_kernel, "sides", [SMEM] + [VMEM] * 7, outs, [pltpu.VMEM((COLS, COLS), F32)])(*args)


def bands(*args):
    return call(bands_kernel, "bands", [VMEM] * 3, [struct(EDGE + RITZ, COLS)] * 2, [])(*args)


def near(ritz_vectors, blocks):
    return call(near_kernel, "near", [VMEM] * 3, [struct(2, RITZ, COLS)], [])(ritz_vectors, *blocks)[0]


def far(place, sums, ritz_vectors, blocks, messages):
    outs = [struct(GROUPS, RITZ)]
    scratch = [pltpu.VMEM((GROUPS, RITZ, COLS), F32)]
    return call(far_kernel, "far", [SMEM] + [VMEM] * 8, outs, scratch)(
        place, sums, ritz_vectors, *blocks, *messages
    )[0]


def update(place, coefficients, ritz_vectors, messages):
    outs = [pltpu.VMEM((RITZ, 2, MAIN // 2, COLS), F32), struct(GROUPS * RITZ, COLS), struct(HALO, COLS)]
    outs += [struct(BLOCK, COLS)] * 3
    scratch = [pltpu.SemaphoreType.DMA((2, RITZ // CHUNK))]
    doubled = jnp.concatenate([coefficients, coefficients], axis=0)
    return call(update_kernel, "update", [SMEM, VMEM, HBM] + [VMEM] * 4, outs, scratch, limit=VMEM_LIMIT)(
        place, doubled, pltpu.with_memory_space_constraint(ritz_vectors.reshape(RITZ, 2, MAIN // 2, COLS), pltpu.HBM), *messages
    )


def own(ritz_vectors, weights, edge):
    return call(own_kernel, "own", [VMEM] * 3, [struct(BLOCK, COLS)], [])(ritz_vectors, weights, edge)[0]


def prolong(place, slots, returned, main, edge, left, right, early=None):
    scratch = [
        pltpu.VMEM((MAIN + 8, 2 * COLS), F32),
        pltpu.VMEM((MAIN + 8, 3 * COLS), F32),
        pltpu.VMEM((2 * COLS, 3 * COLS), BF16),
    ]
    stage = (2, 3, DEPTH, 3 * ROWS, COLS)
    args = (place, *returned, main, edge, left, right)
    specs = [SMEM] + [VMEM] * 6
    kernel = functools.partial(prolong_kernel, slots)
    if early is None:
        return call(kernel, "prolong_early", specs, [pltpu.VMEM(stage, F32)], scratch)(*args)[0]
    scratch += [pltpu.VMEM(stage, F32), pltpu.SemaphoreType.DMA((2, 3)), pltpu.SemaphoreType.DMA((2, 3))]
    outs = [struct(GROUPS * DEPTH, 3 * ROWS, 3 * COLS)]
    return call(kernel, "prolong_late", specs + [VMEM], outs, scratch, [HBM])(*args, early)[0]


def exchange_members(blocks):
    size = lax.axis_size("mem")
    order = (2, 3, 1)
    sent = {shift: lax.ppermute(blocks[shift], "mem", [(i, i ^ shift) for i in range(size)]) for shift in order}
    return [sent[shift] for shift in range(1, size)]


def exchange_sum(value, axes):
    size = lax.axis_size(axes)
    copies = jnp.broadcast_to(value[None], (size,) + value.shape)
    return jnp.sum(lax.all_to_all(copies, axes, 0, 0, tiled=True), axis=0)


def per_device(gradients, ritz_vectors, ritz_values):
    lats, lons = lax.axis_size("lat"), lax.axis_size("lon")
    lat, mem = lax.axis_index("lat"), lax.axis_index("mem")
    place = jnp.stack([mem, jnp.where(lat > 0, 1, 0), jnp.where(lat < lats - 1, 1, 0)]).astype(jnp.int32)

    gradients = gradients.reshape(gradients.shape[1:])
    fine, down, up = edges(gradients)
    over = [(i, (i + 1) % lats) for i in range(lats)]
    under = [((i + 1) % lats, i) for i in range(lats)]
    above = lax.ppermute(down, "lat", over)
    below = lax.ppermute(up, "lat", under)
    held, main, edge, first, last, weights = restrict(fine, ritz_vectors)
    to_left, to_right, main, edge, *blocks = sides(place, above, below, main, edge, first, last, weights)
    right = lax.ppermute(to_left, "lon", [((i + 1) % lons, i) for i in range(lons)])
    left = lax.ppermute(to_right, "lon", [(i, (i + 1) % lons) for i in range(lons)])
    spread = [blocks[0]] + exchange_members(blocks)
    near_sums = near(held, (spread[0], spread[2]))
    left, right, near_sums, *spread = lax.optimization_barrier((left, right, near_sums, *spread))
    down, up = bands(held, left, right)
    above = lax.ppermute(down, "lat", over)
    below = lax.ppermute(up, "lat", under)
    *spread, _, _ = lax.optimization_barrier((*spread, down, up))
    partial = far(place, near_sums, held, spread, (left, right))
    partial = exchange_sum(partial, ("lon", "mem"))
    partial, above, below = lax.optimization_barrier((partial, above, below))
    projections = exchange_sum(partial, "lat")
    cells = GROUPS * DEPTH * ROWS * lats * COLS * lons
    coefficients = (1.0 / ritz_values - 1.0)[None, :] * (projections * (1.0 / cells))

    messages = (above, below, left, right)
    held, weights, own_edge, *sent = update(place, coefficients, ritz_vectors, messages)
    returned = exchange_members([None] + sent)
    mine = own(held, weights, own_edge)
    returned = [mine] + returned
    early = prolong(place, EARLY, [returned[slot] for slot in EARLY], main, edge, left, right)
    output = prolong(place, LATE, [returned[slot] for slot in LATE], main, edge, left, right, early)
    preconditioned = output[None]
    return preconditioned, coefficients


def solution(mesh):
    placed = (P("mem", None, "lat", "lon"), P(None, "mem", "lat", "lon"), P())
    return jax.shard_map(
        per_device,
        mesh=mesh,
        in_specs=placed,
        out_specs=(P("mem", None, "lat", "lon"), P()),
        check_vma=False,
    )
```

```python
import functools

import jax
import jax.numpy as jnp
from jax import lax
from jax.experimental import pallas as pl
from jax.experimental.pallas import tpu as pltpu
from jax.sharding import PartitionSpec as P

F32 = jnp.float32
BF16 = jnp.bfloat16
RITZ = 80
GROUPS = 4
DEPTH = 4
ROWS = 32
COLS = 128
MAIN = DEPTH * ROWS
HALO = 16
BLOCK = MAIN + HALO
LEVELS = GROUPS * DEPTH
BAND = 2 * 3 * LEVELS
EDGE = DEPTH * RITZ
SIDE = RITZ + 4 * GROUPS
CHUNK = 8
PIECE = 16
EARLY = (0, 2)
LATE = (3, 1)
MIB = 1024 * 1024
VMEM_LIMIT = 24 * MIB


def member_index():
    return lax.axis_index("mem")


def has_rows():
    lat = lax.axis_index("lat")
    return [jnp.where(lat > 0, 1.0, 0.0), jnp.where(lat < lax.axis_size("lat") - 1, 1.0, 0.0)]


def iota(shape, dim):
    return lax.broadcasted_iota(jnp.int32, shape, dim)


def diagonal(rows):
    return iota((rows, COLS), 0) == iota((rows, COLS), 1)


def column_to_row(column, mask):
    spread = jnp.broadcast_to(column, mask.shape)
    return jnp.sum(jnp.where(mask, spread, 0.0), axis=0, keepdims=True)


def stack_rows(rows):
    position = iota((8, COLS), 0)
    result = jnp.zeros((8, COLS), F32)
    for index, row in enumerate(rows):
        result = jnp.where(position == index, jnp.broadcast_to(row, (8, COLS)), result)
    return result


def split(value):
    high = value.astype(BF16)
    return high, (value - high.astype(F32)).astype(BF16)


def dot_split(value, weights):
    rows = value.shape[0]
    both = jnp.dot(jnp.concatenate(split(value), axis=0), weights, preferred_element_type=F32)
    return both[:rows] + both[rows:]


def tent_weights(coarse, fine):
    tent = jnp.maximum(3 - jnp.abs(fine - 3 * coarse - 1), 0)
    left = jnp.logical_and(coarse == COLS, fine == 0)
    right = jnp.logical_and(coarse == COLS + 1, fine == 3 * COLS - 1)
    outer = jnp.where(jnp.logical_or(left, right), 1, 0)
    return jnp.where(coarse < COLS, tent, outer)


def edges_kernel(g_ref, f_ref, down_ref, up_ref, sem):
    copies = []
    for part in range(3):
        source = g_ref.at[:, :, pl.ds(COLS * part, COLS)]
        copy = pltpu.make_async_copy(source, f_ref.at[part], sem.at[part])
        copy.start()
        copies.append(copy)
    row = iota((1, 8, COLS), 1)
    plans = (
        (up_ref, 0, jnp.where(row < 4, jnp.where(row == 1, 3, jnp.where(row == 3, 1, 2)), 0), row == 0),
        (
            down_ref,
            3 * ROWS - 8,
            jnp.where(row > 3, jnp.where(row == 6, 3, jnp.where(row == 4, 1, 2)), 0),
            row == 7,
        ),
    )
    for part in range(3):
        copies[part].wait()
        for ref, start, weights, outer in plans:
            fine = f_ref[part, :, start : start + 8, :]
            place = 2 * LEVELS * part
            ref[place : place + LEVELS, :] = jnp.sum(fine * weights.astype(F32), axis=1)
            ref[place + LEVELS : place + 2 * LEVELS, :] = jnp.sum(jnp.where(outer, fine, 0.0), axis=1)


def restrict_kernel(
    f_ref, v_ref, copy_ref, e_ref, h_ref, first_ref, last_ref, w_ref, a_ref, o_ref, m_ref, sem
):
    copies = []
    for start in range(0, RITZ, PIECE):
        place = pl.ds(MAIN * start, MAIN * PIECE)
        copy = pltpu.make_async_copy(v_ref.at[place, :], copy_ref.at[place, :], sem.at[start // PIECE])
        copy.start()
        copies.append(copy)
    fine = iota((3 * COLS, 2 * COLS), 0)
    coarse = iota((3 * COLS, 2 * COLS), 1)
    w_ref[...] = tent_weights(coarse, fine).astype(F32).astype(BF16)
    position = iota((ROWS, COLS), 0)
    o_ref[...] = jnp.zeros_like(o_ref)

    def body(group, carry):
        for part in range(3):
            lanes = slice(COLS * part, COLS * (part + 1))
            for level in range(DEPTH):
                first = f_ref[part, DEPTH * group + level, pl.ds(0, ROWS, stride=3), :]
                middle = f_ref[part, DEPTH * group + level, pl.ds(1, ROWS, stride=3), :]
                third = f_ref[part, DEPTH * group + level, pl.ds(2, ROWS, stride=3), :]
                before = jnp.where(position == 0, 0.0, pltpu.roll(third, 1, 0))
                after = jnp.where(position == ROWS - 1, 0.0, pltpu.roll(first, ROWS - 1, 0))
                high, low = split(before + after + 2.0 * (first + third) + 3.0 * middle)
                start = ROWS * level
                a_ref[start : start + ROWS, lanes] = high
                a_ref[BLOCK + start : BLOCK + start + ROWS, lanes] = low
                o_ref[level : level + 1, lanes] = first[0:1]
                o_ref[DEPTH + level : DEPTH + level + 1, lanes] = third[ROWS - 1 : ROWS]
        high, low = split(o_ref[...])
        a_ref[MAIN:BLOCK, :] = high
        a_ref[BLOCK + MAIN :, :] = low
        both = jnp.dot(a_ref[...], w_ref[...], preferred_element_type=F32)
        coarse = (both[:BLOCK] + both[BLOCK:]) * (1.0 / 81.0)
        e_ref[group] = coarse[:MAIN]
        h_ref[group] = coarse[MAIN : MAIN + 8]
        return carry

    lax.fori_loop(0, GROUPS, body, 0)
    lanes = iota((MAIN, COLS), 1) // 2
    half = RITZ // 2
    for part in range(2):
        packed = jnp.zeros((MAIN, COLS), F32)
        for index in range(half):
            k = half * part + index
            if k % PIECE == 0:
                copies[k // PIECE].wait()
            turned = pltpu.roll(copy_ref[MAIN * k : MAIN * (k + 1), :], 2 * index + 1, 1)
            packed = jnp.where(lanes == index, turned, packed)
        m_ref[...] = jnp.transpose(packed)
        place = slice(half * part, half * (part + 1))
        last_ref[place, :] = m_ref[pl.ds(0, half, stride=2), :]
        first_ref[place, :] = m_ref[pl.ds(1, half, stride=2), :]


def sides_kernel(
    above_ref, below_ref, e_ref, h_ref, first_ref, last_ref, w_ref,
    left_ref, right_ref, e2_ref, h2_ref, x0_ref, x1_ref, x2_ref, x3_ref, m_ref
):
    corner = diagonal(8)
    left_ref[:RITZ, :] = first_ref[...]
    right_ref[:RITZ, :] = last_ref[...]
    position = iota((ROWS, 2 * COLS), 0)
    lanes = iota((MAIN, COLS), 1)
    packed = jnp.zeros((MAIN, COLS), F32)
    corners = ([], [])
    received = []
    for index, ref in enumerate((above_ref, below_ref)):
        parts = [has_rows()[index] * ref[2 * LEVELS * part : 2 * LEVELS * (part + 1), :] for part in range(3)]
        received.append(jnp.concatenate(parts, axis=1))
    received = dot_split(jnp.concatenate(received, axis=0), w_ref[...]) * (1.0 / 81.0)
    for group in range(GROUPS):
        place = slice(DEPTH * group, DEPTH * (group + 1))
        over, above, under, below = [received[LEVELS * i : LEVELS * (i + 1)][place] for i in range(4)]
        for level in range(DEPTH):
            rows = slice(ROWS * level, ROWS * (level + 1))
            tile = e_ref[group, rows, :]
            tile = tile + jnp.where(position == 0, above[level : level + 1, :], 0.0)
            tile = tile + jnp.where(position == ROWS - 1, below[level : level + 1, :], 0.0)
            e2_ref[group, rows, :] = tile
        edge = h_ref[group] + jnp.concatenate([over, under], axis=0)
        h2_ref[group] = edge
        for rows, lane, outer in ((corners[0], 0, COLS), (corners[1], COLS - 1, COLS + 1)):
            for source in (lane, outer):
                rows.append(column_to_row(edge[:, source : source + 1], corner))
        inner = pltpu.roll(e2_ref[group, :, :COLS], 4 * group + 1, 1)
        outer = pltpu.roll(e2_ref[group, :, COLS:], 4 * group + 2, 1)
        packed = jnp.where(lanes // 2 == 2 * group, inner, packed)
        packed = jnp.where(lanes // 2 == 2 * group + 1, outer, packed)
    m_ref[...] = jnp.transpose(packed)
    for ref, row, outer, extra in ((left_ref, 1, 2, corners[0]), (right_ref, 0, 3, corners[1])):
        for pair in range(2):
            rows = []
            for group in (2 * pair, 2 * pair + 1):
                rows.append(m_ref[4 * group + row : 4 * group + row + 1, :])
                rows.append(extra[2 * group])
                rows.append(m_ref[4 * group + outer : 4 * group + outer + 1, :])
                rows.append(extra[2 * group + 1])
            ref[RITZ + 8 * pair : RITZ + 8 * pair + 8, :] = stack_rows(rows)
    for slot, ref in enumerate((x0_ref, x1_ref, x2_ref, x3_ref)):
        group = member_index() ^ slot
        ref[:MAIN] = e2_ref[group, :, :COLS]
        ref[MAIN:] = stack_rows([m_ref[pl.ds(4 * group + 2 + side, 1), :] for side in range(2)])


def bands_kernel(v_ref, left_ref, right_ref, down_ref, up_ref):
    lanes = iota((COLS, COLS), 1)
    for ref, row in ((up_ref, 0), (down_ref, ROWS - 1)):
        corners = jnp.zeros((COLS, COLS), F32)
        for level in range(DEPTH):
            source = ROWS * level + row
            start = RITZ * level
            ref[start : start + RITZ, :] = v_ref[pl.ds(source, RITZ, stride=MAIN), :]
            for side, columns in enumerate((left_ref, right_ref)):
                target = DEPTH * side + level
                column = jnp.concatenate([columns[:RITZ, :], jnp.zeros((COLS - RITZ, COLS), F32)], axis=0)
                turned = pltpu.roll(column, (target - source) % COLS, 1)
                corners = jnp.where(lanes == target, turned, corners)
        ref[EDGE:, :] = jnp.transpose(corners)[:8]


def edge_parts(above_ref, below_ref, left_ref, right_ref):
    keep = has_rows()
    parts = []
    for index, source in enumerate((above_ref, below_ref)):
        for level in range(DEPTH):
            parts.append(keep[index] * source[RITZ * level : RITZ * (level + 1), :])
    parts += [left_ref[:RITZ, :], right_ref[:RITZ, :]]
    corners = [keep[index] * source[EDGE:, :RITZ] for index, source in enumerate((above_ref, below_ref))]
    return parts, corners


def lane_sums(v_ref, blocks, left_ref, right_ref, s_ref):
    def body(step, carry):
        base = pl.multiple_of(step * CHUNK, CHUNK)
        sums = [[jnp.zeros((8, COLS), F32) for _ in range(CHUNK)] for _ in blocks]
        for tile in range(MAIN // 8):
            fields = [block[8 * tile : 8 * tile + 8, :] for block in blocks]
            for k in range(CHUNK):
                vector = v_ref[pl.ds(pl.multiple_of((base + k) * MAIN + 8 * tile, 8), 8), :]
                for member, field in enumerate(fields):
                    sums[member][k] = sums[member][k] + vector * field
        for member, block in enumerate(blocks):
            total = stack_rows([jnp.sum(value, axis=0, keepdims=True) for value in sums[member]])
            for side, column_ref in enumerate((left_ref, right_ref)):
                total = total + column_ref[pl.ds(base, CHUNK), :] * block[MAIN + side : MAIN + side + 1, :]
            s_ref[pl.ds(COLS * member + base, CHUNK), :] = total
        return carry

    lax.fori_loop(0, RITZ // CHUNK, body, 0)
    high, low = split(s_ref[...])
    rest = (s_ref[...] - high.astype(F32) - low.astype(F32)).astype(BF16)
    ones = jnp.ones((8, 3 * COLS), BF16)
    parts = jnp.concatenate([high, low, rest], axis=1)
    sums = lax.dot_general(ones, parts, (((1,), (1,)), ((), ())), preferred_element_type=F32)
    return [sums[0:1, COLS * member : COLS * member + RITZ] for member in range(len(blocks))]


def near_kernel(v_ref, c0_ref, c2_ref, left_ref, right_ref, p_ref, s_ref):
    for index, row in enumerate(lane_sums(v_ref, (c0_ref, c2_ref), left_ref, right_ref, s_ref)):
        p_ref[index : index + 1, :] = row


def far_kernel(near_ref, v_ref, c3_ref, c1_ref, left_ref, right_ref, p_ref, s_ref):
    rows = lane_sums(v_ref, (c3_ref, c1_ref), left_ref, right_ref, s_ref)
    for slot, row in zip((0, 2, 3, 1), [near_ref[0:1, :], near_ref[1:2, :]] + rows):
        p_ref[pl.ds(member_index() ^ slot, 1), :] = row


def exact_dot(left, right, dims):
    return lax.dot_general(
        left, right, (dims, ((), ())), precision=lax.Precision.HIGHEST, preferred_element_type=F32
    )


def weighted_sums(v_ref, b_ref, slots, prepare):
    half = MAIN // 2
    results = []
    for part in range(2):

        def body(index, sums, part=part):
            prepare(part, index)
            for offset in range(CHUNK):
                k = index * CHUNK + offset
                vector = v_ref[k, part]
                sums = [
                    value + b_ref[pl.ds(RITZ * member + k, 1), :] * vector for value, member in zip(sums, slots)
                ]
            return tuple(sums)

        zeros = tuple(jnp.zeros((half, COLS), F32) for _ in slots)
        results.append(lax.fori_loop(0, RITZ // CHUNK, body, zeros))
    return results


def update_kernel(
    c_ref, v_hbm_ref, above_ref, below_ref, left_ref, right_ref,
    v_ref, b_ref, edge_ref, u1_ref, u2_ref, u3_ref, sem
):
    me = member_index()
    outs = (None, u1_ref, u2_ref, u3_ref)
    pieces = RITZ // CHUNK

    def copy(part, piece):
        source = v_hbm_ref.at[pl.ds(piece * CHUNK, CHUNK), part]
        return pltpu.make_async_copy(source, v_ref.at[pl.ds(piece * CHUNK, CHUNK), part], sem.at[part, piece])

    for part in range(2):
        for piece in range(pieces):
            copy(part, piece).start()
    coefficients = c_ref[...]
    for member in range(GROUPS):
        chosen = jnp.where(iota((8, COLS), 0) == (me ^ member), 1.0, 0.0)
        b_ref[RITZ * member : RITZ * (member + 1), :] = exact_dot(coefficients, chosen, ((0,), (0,)))
    swap = jnp.where(iota((8, 8), 1) == (me ^ iota((8, 8), 0)), 1.0, 0.0)
    ordered = exact_dot(swap, coefficients, ((1,), (0,)))
    parts, corners = edge_parts(above_ref, below_ref, left_ref, right_ref)
    edge = exact_dot(ordered, jnp.concatenate(parts, axis=1), ((1,), (0,)))
    corners = [exact_dot(ordered, corner, ((1,), (1,))) for corner in corners]
    places = list(range(2 * DEPTH)) + [8, 10]
    for member in range(GROUPS):
        ref, start = (outs[member], MAIN) if member else (edge_ref, 0)
        ref[start + 8 : start + HALO, :] = jnp.zeros((HALO - 8, COLS), F32)
        for index, place in enumerate(places):
            row = edge[member : member + 1, COLS * index : COLS * (index + 1)]
            ref[start + place : start + place + 1, :] = row
        for index, place in enumerate((9, 11)):
            ref[start + place : start + place + 1, :8] = corners[index][member : member + 1, :]

    def prepare(part, index):
        copy(part, index).wait()

    half = MAIN // 2
    for part, sums in enumerate(weighted_sums(v_ref, b_ref, (1, 2, 3), prepare)):
        for member, value in zip((1, 2, 3), sums):
            outs[member][half * part : half * (part + 1), :] = value


def own_kernel(v_ref, b_ref, edge_ref, u0_ref):
    half = MAIN // 2
    for part, sums in enumerate(weighted_sums(v_ref, b_ref, (0,), lambda part, index: None)):
        u0_ref[half * part : half * (part + 1), :] = sums[0]
    u0_ref[MAIN:, :] = edge_ref[...]


def write_group(o_ref, m_ref, group, index, sem):
    copies = []
    for part in range(3):
        target = o_ref.at[pl.ds(DEPTH * group, DEPTH), :, pl.ds(COLS * part, COLS)]
        copy = pltpu.make_async_copy(m_ref.at[index, part], target, sem.at[index, part])
        copy.start()
        copies.append(copy)
    return copies


def prolong_kernel(slots, ra_ref, rb_ref, e2_ref, h2_ref, left_ref, right_ref, *refs):
    early_ref = None
    copies = []
    if len(refs) == 4:
        m_ref, a_ref, f_ref, z_ref = refs
    else:
        early_ref, o_ref, a_ref, f_ref, z_ref, m_ref, early_sem, sem = refs
        for index, slot in enumerate(EARLY):
            copies += write_group(o_ref, early_ref, member_index() ^ slot, index, early_sem)
    coarse = iota((2 * COLS, 3 * COLS), 0)
    fine = iota((2 * COLS, 3 * COLS), 1)
    coarse = jnp.where(coarse == COLS + 2, 0, jnp.where(coarse == COLS + 3, COLS - 1, coarse))
    z_ref[...] = tent_weights(coarse, fine).astype(F32).astype(BF16)
    row = iota((8, COLS), 0)
    keep = jnp.where(row < DEPTH, *has_rows())
    outer_lanes = iota((MAIN, COLS), 1) < 4
    position = iota((ROWS, 3 * COLS), 0)
    for index, (slot, r_ref) in enumerate(zip(slots, (ra_ref, rb_ref))):
        group = member_index() ^ slot
        start = RITZ + 4 * group
        outer = [r_ref[MAIN + 8 + kind : MAIN + 9 + kind, :] for kind in range(4)]
        first_half = iota((1, COLS), 1) < DEPTH
        beyond = (
            (outer[0], outer[2]),
            (
                jnp.where(first_half, outer[1], pltpu.roll(outer[3], DEPTH, 1)),
                jnp.where(first_half, pltpu.roll(outer[1], COLS - DEPTH, 1), outer[3]),
            ),
        )
        rows = []
        for kind in range(2):
            for ref, value in zip((left_ref, right_ref), beyond[kind]):
                rows.append(ref[pl.ds(start + kind, 1), :] + value)
            for ref in (left_ref, right_ref):
                rows.append(ref[pl.ds(start + 2 + kind, 1), :])
        stacked = jnp.concatenate([stack_rows(rows), jnp.zeros((COLS - 8, COLS), F32)], axis=0)
        turned = jnp.transpose(stacked)
        corners = pltpu.roll(turned[:8], COLS - 4, 1)
        a_ref[:MAIN, :COLS] = e2_ref[group, :, :COLS] + r_ref[:MAIN, :]
        a_ref[:MAIN, COLS:] = e2_ref[group, :, COLS:] + jnp.where(outer_lanes, turned, 0.0)
        a_ref[MAIN:, :COLS] = (h2_ref[group, :, :COLS] + r_ref[MAIN : MAIN + 8, :]) * keep
        a_ref[MAIN:, COLS:] = (h2_ref[group, :, COLS:] + jnp.where(outer_lanes[:8], corners, 0.0)) * keep
        f_ref[...] = dot_split(a_ref[...], z_ref[...])
        for level in range(DEPTH):
            center = f_ref[ROWS * level : ROWS * (level + 1), :]
            above = f_ref[MAIN + level : MAIN + level + 1, :]
            below = f_ref[MAIN + DEPTH + level : MAIN + DEPTH + level + 1, :]
            before = jnp.where(position == 0, above, pltpu.roll(center, 1, 0))
            after = jnp.where(position == ROWS - 1, below, pltpu.roll(center, ROWS - 1, 0))
            fine = ((2.0 * center + before) * (1.0 / 9.0), center * (1.0 / 3.0), (2.0 * center + after) * (1.0 / 9.0))
            for part in range(3):
                lanes = slice(COLS * part, COLS * (part + 1))
                for offset, value in enumerate(fine):
                    m_ref[index, part, level, pl.ds(offset, ROWS, stride=3), :] = value[:, lanes]
        if early_ref is not None:
            copies += write_group(o_ref, m_ref, group, index, sem)
    for copy in copies:
        copy.wait()


def struct(*shape):
    return jax.ShapeDtypeStruct(shape, F32)


VMEM = pl.BlockSpec(memory_space=pltpu.VMEM)
HBM = pl.BlockSpec(memory_space=pltpu.HBM)
FIELD = (GROUPS, MAIN, 2 * COLS)
RIM = (GROUPS, 8, 2 * COLS)


def call(kernel, name, ins, outs, scratch, out_specs=None):
    return pl.pallas_call(
        kernel,
        in_specs=ins,
        out_specs=out_specs or [VMEM] * len(outs),
        out_shape=outs,
        scratch_shapes=scratch,
        compiler_params=pltpu.CompilerParams(vmem_limit_bytes=VMEM_LIMIT),
        name=name,
    )


def pinned(value):
    return pltpu.with_memory_space_constraint(value, pltpu.HBM)


def edges(gradients):
    scratch = [pltpu.SemaphoreType.DMA((3,))]
    outs = [pltpu.VMEM((3, LEVELS, 3 * ROWS, COLS), F32)] + [struct(BAND, COLS)] * 2
    gradients = pinned(gradients)
    return call(edges_kernel, "edges", [HBM], outs, scratch)(gradients)


def restrict(fine, ritz_vectors):
    scratch = [
        pltpu.VMEM((2 * BLOCK, 3 * COLS), BF16),
        pltpu.VMEM((HALO, 3 * COLS), F32),
        pltpu.VMEM((COLS, COLS), F32),
        pltpu.SemaphoreType.DMA((RITZ // PIECE,)),
    ]
    outs = [pltpu.VMEM((RITZ * MAIN, COLS), F32)]
    outs += [struct(*FIELD), struct(*RIM)] + [struct(RITZ, COLS)] * 2
    outs += [pltpu.VMEM((3 * COLS, 2 * COLS), BF16)]
    flat = pinned(ritz_vectors.reshape(RITZ * MAIN, COLS))
    return call(restrict_kernel, "restrict", [VMEM, HBM], outs, scratch)(fine, flat)


def sides(*args):
    outs = [struct(SIDE, COLS)] * 2 + [struct(*FIELD), struct(*RIM)] + [struct(MAIN + 8, COLS)] * 4
    return call(sides_kernel, "sides", [VMEM] * 7, outs, [pltpu.VMEM((COLS, COLS), F32)])(*args)


def bands(*args):
    return call(bands_kernel, "bands", [VMEM] * 3, [struct(EDGE + 8, COLS)] * 2, [])(*args)


def near(held, blocks, columns):
    outs, scratch = [struct(2, RITZ)], [pltpu.VMEM((2 * COLS, COLS), F32)]
    return call(near_kernel, "near", [VMEM] * 5, outs, scratch)(held, *blocks, *columns)[0]


def far(sums, held, blocks, columns):
    outs, scratch = [struct(GROUPS, RITZ)], [pltpu.VMEM((2 * COLS, COLS), F32)]
    return call(far_kernel, "far", [VMEM] * 6, outs, scratch)(sums, held, *blocks, *columns)[0]


def update(coefficients, ritz_vectors, messages):
    outs = [pltpu.VMEM((RITZ, 2, MAIN // 2, COLS), F32), struct(GROUPS * RITZ, COLS), struct(HALO, COLS)]
    outs += [struct(BLOCK, COLS)] * 3
    scratch = [pltpu.SemaphoreType.DMA((2, RITZ // CHUNK))]
    doubled = jnp.concatenate([coefficients, coefficients], axis=0)
    return call(update_kernel, "update", [VMEM, HBM] + [VMEM] * 4, outs, scratch)(
        doubled, pinned(ritz_vectors.reshape(RITZ, 2, MAIN // 2, COLS)), *messages
    )


def own(*args):
    return call(own_kernel, "own", [VMEM] * 3, [struct(BLOCK, COLS)], [])(*args)[0]


def prolong(slots, returned, main, edge, left, right, early=None):
    scratch = [
        pltpu.VMEM((MAIN + 8, 2 * COLS), F32),
        pltpu.VMEM((MAIN + 8, 3 * COLS), F32),
        pltpu.VMEM((2 * COLS, 3 * COLS), BF16),
    ]
    stage = (2, 3, DEPTH, 3 * ROWS, COLS)
    args = (*returned, main, edge, left, right)
    specs = [VMEM] * 6
    kernel = functools.partial(prolong_kernel, slots)
    if early is None:
        return call(kernel, "prolong_early", specs, [pltpu.VMEM(stage, F32)], scratch)(*args)[0]
    scratch += [pltpu.VMEM(stage, F32), pltpu.SemaphoreType.DMA((2, 3)), pltpu.SemaphoreType.DMA((2, 3))]
    outs = [jax.ShapeDtypeStruct((GROUPS * DEPTH, 3 * ROWS, 3 * COLS), F32)]
    return call(kernel, "prolong_late", specs + [VMEM], outs, scratch, [HBM])(*args, early)[0]


def exchange_members(blocks):
    size = lax.axis_size("mem")
    order = (2, 3, 1)
    sent = {shift: lax.ppermute(blocks[shift], "mem", [(i, i ^ shift) for i in range(size)]) for shift in order}
    return [sent[shift] for shift in range(1, size)]


def exchange_sum(value, axes):
    size = lax.axis_size(axes)
    copies = jnp.broadcast_to(value[None], (size,) + value.shape)
    return jnp.sum(lax.all_to_all(copies, axes, 0, 0, tiled=True), axis=0)


def per_device(gradients, ritz_vectors, ritz_values):
    lats, lons = lax.axis_size("lat"), lax.axis_size("lon")

    gradients = gradients.reshape(gradients.shape[1:])
    fine, down, up = edges(gradients)
    over = [(i, (i + 1) % lats) for i in range(lats)]
    under = [((i + 1) % lats, i) for i in range(lats)]
    above = lax.ppermute(down, "lat", over)
    below = lax.ppermute(up, "lat", under)
    held, main, edge, first, last, weights = restrict(fine, ritz_vectors)
    to_left, to_right, main, edge, *blocks = sides(above, below, main, edge, first, last, weights)
    right = lax.ppermute(to_left, "lon", [((i + 1) % lons, i) for i in range(lons)])
    left = lax.ppermute(to_right, "lon", [(i, (i + 1) % lons) for i in range(lons)])
    spread = [blocks[0]] + exchange_members(blocks)
    near_sums = near(held, (spread[0], spread[2]), (left, right))
    left, right, near_sums, *spread = lax.optimization_barrier((left, right, near_sums, *spread))
    down, up = bands(held, left, right)
    above = lax.ppermute(down, "lat", over)
    below = lax.ppermute(up, "lat", under)
    *spread, _, _ = lax.optimization_barrier((*spread, down, up))
    partial = far(near_sums, held, (spread[3], spread[1]), (left, right))
    cells = GROUPS * DEPTH * ROWS * lats * COLS * lons
    factors = (1.0 / ritz_values - 1.0) * (1.0 / cells)
    partial, factors = lax.optimization_barrier((partial, factors))
    for shift in (1, 2):
        partial = partial + lax.ppermute(partial, "mem", [(i, i ^ shift) for i in range(4)])
    coefficients = factors[None, :] * exchange_sum(partial, ("lat", "lon"))
    messages = (above, below, left, right)
    held, weights, own_edge, *sent = update(coefficients, ritz_vectors, messages)
    returned = exchange_members([None] + sent)
    mine = own(held, weights, own_edge)
    returned = [mine] + returned
    early = prolong(EARLY, [returned[slot] for slot in EARLY], main, edge, left, right)
    output = prolong(LATE, [returned[slot] for slot in LATE], main, edge, left, right, early)
    preconditioned = output[None]
    return preconditioned, coefficients


def solution(mesh):
    placed = (P("mem", None, "lat", "lon"), P(None, "mem", "lat", "lon"), P())
    return jax.shard_map(
        per_device,
        mesh=mesh,
        in_specs=placed,
        out_specs=(P("mem", None, "lat", "lon"), P()),
        check_vma=False,
    )
```

```python
import functools

import jax
import jax.numpy as jnp
from jax import lax
from jax.experimental import pallas as pl
from jax.experimental.pallas import tpu as pltpu
from jax.sharding import PartitionSpec as P

F32 = jnp.float32
BF16 = jnp.bfloat16
RITZ = 80
GROUPS = 4
DEPTH = 4
ROWS = 32
COLS = 128
MAIN = DEPTH * ROWS
HALO = 16
BLOCK = MAIN + HALO
LEVELS = GROUPS * DEPTH
BAND = 2 * 3 * LEVELS
EDGE = DEPTH * RITZ
SIDE = RITZ + 4 * GROUPS
CHUNK = 8
PIECE = 16
EARLY = (0, 2)
LATE = (3, 1)
MIB = 1024 * 1024
VMEM_LIMIT = 24 * MIB


def member_index():
    return lax.axis_index("mem")


def has_rows():
    lat = lax.axis_index("lat")
    return [jnp.where(lat > 0, 1.0, 0.0), jnp.where(lat < lax.axis_size("lat") - 1, 1.0, 0.0)]


def iota(shape, dim):
    return lax.broadcasted_iota(jnp.int32, shape, dim)


def diagonal(rows):
    return iota((rows, COLS), 0) == iota((rows, COLS), 1)


def column_to_row(column, mask):
    spread = jnp.broadcast_to(column, mask.shape)
    return jnp.sum(jnp.where(mask, spread, 0.0), axis=0, keepdims=True)


def stack_rows(rows):
    position = iota((8, COLS), 0)
    result = jnp.zeros((8, COLS), F32)
    for index, row in enumerate(rows):
        result = jnp.where(position == index, jnp.broadcast_to(row, (8, COLS)), result)
    return result


def split(value):
    high = value.astype(BF16)
    return high, (value - high.astype(F32)).astype(BF16)


def dot_split(value, weights):
    rows = value.shape[0]
    both = jnp.dot(jnp.concatenate(split(value), axis=0), weights, preferred_element_type=F32)
    return both[:rows] + both[rows:]


def tent_weights(coarse, fine):
    tent = jnp.maximum(3 - jnp.abs(fine - 3 * coarse - 1), 0)
    left = jnp.logical_and(coarse == COLS, fine == 0)
    right = jnp.logical_and(coarse == COLS + 1, fine == 3 * COLS - 1)
    outer = jnp.where(jnp.logical_or(left, right), 1, 0)
    return jnp.where(coarse < COLS, tent, outer)


def edges_kernel(g_ref, f_ref, down_ref, up_ref, sem):
    copies = []
    for part in range(3):
        source = g_ref.at[:, :, pl.ds(COLS * part, COLS)]
        copy = pltpu.make_async_copy(source, f_ref.at[part], sem.at[part])
        copy.start()
        copies.append(copy)
    row = iota((1, 8, COLS), 1)
    plans = (
        (up_ref, 0, jnp.where(row < 4, jnp.where(row == 1, 3, jnp.where(row == 3, 1, 2)), 0), row == 0),
        (
            down_ref,
            3 * ROWS - 8,
            jnp.where(row > 3, jnp.where(row == 6, 3, jnp.where(row == 4, 1, 2)), 0),
            row == 7,
        ),
    )
    for part in range(3):
        copies[part].wait()
        for ref, start, weights, outer in plans:
            fine = f_ref[part, :, start : start + 8, :]
            place = 2 * LEVELS * part
            ref[place : place + LEVELS, :] = jnp.sum(fine * weights.astype(F32), axis=1)
            ref[place + LEVELS : place + 2 * LEVELS, :] = jnp.sum(jnp.where(outer, fine, 0.0), axis=1)


def restrict_kernel(
    f_ref, v_ref, copy_ref, e_ref, h_ref, first_ref, last_ref, w_ref, a_ref, o_ref, m_ref, sem
):
    copies = []
    for start in range(0, RITZ, PIECE):
        place = pl.ds(MAIN * start, MAIN * PIECE)
        copy = pltpu.make_async_copy(v_ref.at[place, :], copy_ref.at[place, :], sem.at[start // PIECE])
        copy.start()
        copies.append(copy)
    fine = iota((3 * COLS, 2 * COLS), 0)
    coarse = iota((3 * COLS, 2 * COLS), 1)
    w_ref[...] = tent_weights(coarse, fine).astype(F32).astype(BF16)
    position = iota((ROWS, COLS), 0)
    o_ref[...] = jnp.zeros_like(o_ref)

    def body(group, carry):
        for part in range(3):
            lanes = slice(COLS * part, COLS * (part + 1))
            for level in range(DEPTH):
                first = f_ref[part, DEPTH * group + level, pl.ds(0, ROWS, stride=3), :]
                middle = f_ref[part, DEPTH * group + level, pl.ds(1, ROWS, stride=3), :]
                third = f_ref[part, DEPTH * group + level, pl.ds(2, ROWS, stride=3), :]
                before = jnp.where(position == 0, 0.0, pltpu.roll(third, 1, 0))
                after = jnp.where(position == ROWS - 1, 0.0, pltpu.roll(first, ROWS - 1, 0))
                high, low = split(before + after + 2.0 * (first + third) + 3.0 * middle)
                start = ROWS * level
                a_ref[start : start + ROWS, lanes] = high
                a_ref[BLOCK + start : BLOCK + start + ROWS, lanes] = low
                o_ref[level : level + 1, lanes] = first[0:1]
                o_ref[DEPTH + level : DEPTH + level + 1, lanes] = third[ROWS - 1 : ROWS]
        high, low = split(o_ref[...])
        a_ref[MAIN:BLOCK, :] = high
        a_ref[BLOCK + MAIN :, :] = low
        both = jnp.dot(a_ref[...], w_ref[...], preferred_element_type=F32)
        coarse = (both[:BLOCK] + both[BLOCK:]) * (1.0 / 81.0)
        e_ref[group] = coarse[:MAIN]
        h_ref[group] = coarse[MAIN : MAIN + 8]
        return carry

    lax.fori_loop(0, GROUPS, body, 0)
    lanes = iota((MAIN, COLS), 1) // 2
    half = RITZ // 2
    for part in range(2):
        packed = jnp.zeros((MAIN, COLS), F32)
        for index in range(half):
            k = half * part + index
            if k % PIECE == 0:
                copies[k // PIECE].wait()
            turned = pltpu.roll(copy_ref[MAIN * k : MAIN * (k + 1), :], 2 * index + 1, 1)
            packed = jnp.where(lanes == index, turned, packed)
        m_ref[...] = jnp.transpose(packed)
        place = slice(half * part, half * (part + 1))
        last_ref[place, :] = m_ref[pl.ds(0, half, stride=2), :]
        first_ref[place, :] = m_ref[pl.ds(1, half, stride=2), :]


def sides_kernel(
    above_ref, below_ref, e_ref, h_ref, first_ref, last_ref, w_ref,
    left_ref, right_ref, e2_ref, h2_ref, x0_ref, x1_ref, x2_ref, x3_ref, m_ref
):
    corner = diagonal(8)
    left_ref[:RITZ, :] = first_ref[...]
    right_ref[:RITZ, :] = last_ref[...]
    position = iota((ROWS, 2 * COLS), 0)
    lanes = iota((MAIN, COLS), 1)
    packed = jnp.zeros((MAIN, COLS), F32)
    corners = ([], [])
    received = []
    for index, ref in enumerate((above_ref, below_ref)):
        parts = [has_rows()[index] * ref[2 * LEVELS * part : 2 * LEVELS * (part + 1), :] for part in range(3)]
        received.append(jnp.concatenate(parts, axis=1))
    received = dot_split(jnp.concatenate(received, axis=0), w_ref[...]) * (1.0 / 81.0)
    for group in range(GROUPS):
        place = slice(DEPTH * group, DEPTH * (group + 1))
        over, above, under, below = [received[LEVELS * i : LEVELS * (i + 1)][place] for i in range(4)]
        for level in range(DEPTH):
            rows = slice(ROWS * level, ROWS * (level + 1))
            tile = e_ref[group, rows, :]
            tile = tile + jnp.where(position == 0, above[level : level + 1, :], 0.0)
            tile = tile + jnp.where(position == ROWS - 1, below[level : level + 1, :], 0.0)
            e2_ref[group, rows, :] = tile
        edge = h_ref[group] + jnp.concatenate([over, under], axis=0)
        h2_ref[group] = edge
        for rows, lane, outer in ((corners[0], 0, COLS), (corners[1], COLS - 1, COLS + 1)):
            for source in (lane, outer):
                rows.append(column_to_row(edge[:, source : source + 1], corner))
        inner = pltpu.roll(e2_ref[group, :, :COLS], 4 * group + 1, 1)
        outer = pltpu.roll(e2_ref[group, :, COLS:], 4 * group + 2, 1)
        packed = jnp.where(lanes // 2 == 2 * group, inner, packed)
        packed = jnp.where(lanes // 2 == 2 * group + 1, outer, packed)
    m_ref[...] = jnp.transpose(packed)
    for ref, row, outer, extra in ((left_ref, 1, 2, corners[0]), (right_ref, 0, 3, corners[1])):
        for pair in range(2):
            rows = []
            for group in (2 * pair, 2 * pair + 1):
                rows.append(m_ref[4 * group + row : 4 * group + row + 1, :])
                rows.append(extra[2 * group])
                rows.append(m_ref[4 * group + outer : 4 * group + outer + 1, :])
                rows.append(extra[2 * group + 1])
            ref[RITZ + 8 * pair : RITZ + 8 * pair + 8, :] = stack_rows(rows)
    for slot, ref in enumerate((x0_ref, x1_ref, x2_ref, x3_ref)):
        group = member_index() ^ slot
        ref[:MAIN] = e2_ref[group, :, :COLS]
        ref[MAIN:] = stack_rows([m_ref[pl.ds(4 * group + 2 + side, 1), :] for side in range(2)])


def bands_kernel(v_ref, left_ref, right_ref, down_ref, up_ref):
    lanes = iota((COLS, COLS), 1)
    for ref, row in ((up_ref, 0), (down_ref, ROWS - 1)):
        corners = jnp.zeros((COLS, COLS), F32)
        for level in range(DEPTH):
            source = ROWS * level + row
            start = RITZ * level
            ref[start : start + RITZ, :] = v_ref[pl.ds(source, RITZ, stride=MAIN), :]
            for side, columns in enumerate((left_ref, right_ref)):
                target = DEPTH * side + level
                column = jnp.concatenate([columns[:RITZ, :], jnp.zeros((COLS - RITZ, COLS), F32)], axis=0)
                turned = pltpu.roll(column, (target - source) % COLS, 1)
                corners = jnp.where(lanes == target, turned, corners)
        ref[EDGE:, :] = jnp.transpose(corners)[:8]


def edge_parts(above_ref, below_ref, left_ref, right_ref):
    keep = has_rows()
    parts = []
    for index, source in enumerate((above_ref, below_ref)):
        for level in range(DEPTH):
            parts.append(keep[index] * source[RITZ * level : RITZ * (level + 1), :])
    parts += [left_ref[:RITZ, :], right_ref[:RITZ, :]]
    corners = [keep[index] * source[EDGE:, :RITZ] for index, source in enumerate((above_ref, below_ref))]
    return parts, corners


def lane_sums(v_ref, blocks, left_ref, right_ref, s_ref):
    def body(step, carry):
        base = pl.multiple_of(step * CHUNK, CHUNK)
        sums = [[jnp.zeros((8, COLS), F32) for _ in range(CHUNK)] for _ in blocks]
        for tile in range(MAIN // 8):
            fields = [block[8 * tile : 8 * tile + 8, :] for block in blocks]
            for k in range(CHUNK):
                vector = v_ref[pl.ds(pl.multiple_of((base + k) * MAIN + 8 * tile, 8), 8), :]
                for member, field in enumerate(fields):
                    sums[member][k] = sums[member][k] + vector * field
        for member, block in enumerate(blocks):
            total = stack_rows([jnp.sum(value, axis=0, keepdims=True) for value in sums[member]])
            for side, column_ref in enumerate((left_ref, right_ref)):
                total = total + column_ref[pl.ds(base, CHUNK), :] * block[MAIN + side : MAIN + side + 1, :]
            s_ref[pl.ds(COLS * member + base, CHUNK), :] = total
        return carry

    lax.fori_loop(0, RITZ // CHUNK, body, 0)
    high, low = split(s_ref[...])
    rest = (s_ref[...] - high.astype(F32) - low.astype(F32)).astype(BF16)
    ones = jnp.ones((8, 3 * COLS), BF16)
    parts = jnp.concatenate([high, low, rest], axis=1)
    sums = lax.dot_general(ones, parts, (((1,), (1,)), ((), ())), preferred_element_type=F32)
    return [sums[0:1, COLS * member : COLS * member + RITZ] for member in range(len(blocks))]


def near_kernel(v_ref, c0_ref, c2_ref, left_ref, right_ref, p_ref, s_ref):
    for index, row in enumerate(lane_sums(v_ref, (c0_ref, c2_ref), left_ref, right_ref, s_ref)):
        p_ref[index : index + 1, :] = row


def far_kernel(near_ref, v_ref, c3_ref, c1_ref, left_ref, right_ref, p_ref, s_ref):
    rows = lane_sums(v_ref, (c3_ref, c1_ref), left_ref, right_ref, s_ref)
    for slot, row in zip((0, 2, 3, 1), [near_ref[0:1, :], near_ref[1:2, :]] + rows):
        p_ref[pl.ds(member_index() ^ slot, 1), :] = row


def exact_dot(left, right, dims):
    return lax.dot_general(
        left, right, (dims, ((), ())), precision=lax.Precision.HIGHEST, preferred_element_type=F32
    )


def weighted_sums(v_ref, b_ref, slots, prepare):
    half = MAIN // 2
    results = []
    for part in range(2):

        def body(index, sums, part=part):
            prepare(part, index)
            for offset in range(CHUNK):
                k = index * CHUNK + offset
                vector = v_ref[k, part]
                sums = [
                    value + b_ref[pl.ds(RITZ * member + k, 1), :] * vector for value, member in zip(sums, slots)
                ]
            return tuple(sums)

        zeros = tuple(jnp.zeros((half, COLS), F32) for _ in slots)
        results.append(lax.fori_loop(0, RITZ // CHUNK, body, zeros))
    return results


def update_kernel(
    c_ref, v_hbm_ref, above_ref, below_ref, left_ref, right_ref,
    v_ref, b_ref, edge_ref, u1_ref, u2_ref, u3_ref, sem
):
    me = member_index()
    outs = (None, u1_ref, u2_ref, u3_ref)
    pieces = RITZ // CHUNK

    def copy(part, piece):
        source = v_hbm_ref.at[pl.ds(piece * CHUNK, CHUNK), part]
        return pltpu.make_async_copy(source, v_ref.at[pl.ds(piece * CHUNK, CHUNK), part], sem.at[part, piece])

    for part in range(2):
        for piece in range(pieces):
            copy(part, piece).start()
    coefficients = c_ref[...]
    places = [iota((8, COLS), 0) == (me ^ member) for member in range(GROUPS)]
    chosen = jnp.concatenate([jnp.where(place, 1.0, 0.0) for place in places], axis=1)
    spread = exact_dot(coefficients, chosen, ((0,), (0,)))
    for member in range(GROUPS):
        b_ref[RITZ * member : RITZ * (member + 1), :] = spread[:, COLS * member : COLS * (member + 1)]
    swap = jnp.where(iota((8, 8), 1) == (me ^ iota((8, 8), 0)), 1.0, 0.0)
    ordered = exact_dot(swap, coefficients, ((1,), (0,)))
    parts, corners = edge_parts(above_ref, below_ref, left_ref, right_ref)
    edge = exact_dot(ordered, jnp.concatenate(parts, axis=1), ((1,), (0,)))
    corners = [exact_dot(ordered, corner, ((1,), (1,))) for corner in corners]
    places = list(range(2 * DEPTH)) + [8, 10]
    for member in range(GROUPS):
        ref, start = (outs[member], MAIN) if member else (edge_ref, 0)
        ref[start + 8 : start + HALO, :] = jnp.zeros((HALO - 8, COLS), F32)
        for index, place in enumerate(places):
            row = edge[member : member + 1, COLS * index : COLS * (index + 1)]
            ref[start + place : start + place + 1, :] = row
        for index, place in enumerate((9, 11)):
            ref[start + place : start + place + 1, :8] = corners[index][member : member + 1, :]

    def prepare(part, index):
        copy(part, index).wait()

    half = MAIN // 2
    for part, sums in enumerate(weighted_sums(v_ref, b_ref, (1, 2, 3), prepare)):
        for member, value in zip((1, 2, 3), sums):
            outs[member][half * part : half * (part + 1), :] = value


def own_kernel(v_ref, b_ref, edge_ref, u0_ref):
    half = MAIN // 2
    for part, sums in enumerate(weighted_sums(v_ref, b_ref, (0,), lambda part, index: None)):
        u0_ref[half * part : half * (part + 1), :] = sums[0]
    u0_ref[MAIN:, :] = edge_ref[...]


def write_group(o_ref, m_ref, group, index, sem):
    copies = []
    for part in range(3):
        target = o_ref.at[pl.ds(DEPTH * group, DEPTH), :, pl.ds(COLS * part, COLS)]
        copy = pltpu.make_async_copy(m_ref.at[index, part], target, sem.at[index, part])
        copy.start()
        copies.append(copy)
    return copies


def prolong_kernel(slots, ra_ref, rb_ref, e2_ref, h2_ref, left_ref, right_ref, *refs):
    early_ref = None
    copies = []
    if len(refs) == 4:
        m_ref, a_ref, f_ref, z_ref = refs
    else:
        early_ref, o_ref, a_ref, f_ref, z_ref, m_ref, early_sem, sem = refs
        for index, slot in enumerate(EARLY):
            copies += write_group(o_ref, early_ref, member_index() ^ slot, index, early_sem)
    coarse = iota((2 * COLS, 3 * COLS), 0)
    fine = iota((2 * COLS, 3 * COLS), 1)
    coarse = jnp.where(coarse == COLS + 2, 0, jnp.where(coarse == COLS + 3, COLS - 1, coarse))
    a_ref[MAIN + 8 :, :] = jnp.zeros((BLOCK - MAIN - 8, 2 * COLS), F32)
    z_ref[...] = tent_weights(coarse, fine).astype(F32).astype(BF16)
    row = iota((8, COLS), 0)
    keep = jnp.where(row < DEPTH, *has_rows())
    outer_lanes = iota((MAIN, COLS), 1) < 4
    position = iota((ROWS, 3 * COLS), 0)
    for index, (slot, r_ref) in enumerate(zip(slots, (ra_ref, rb_ref))):
        group = member_index() ^ slot
        start = RITZ + 4 * group
        outer = [r_ref[MAIN + 8 + kind : MAIN + 9 + kind, :] for kind in range(4)]
        first_half = iota((1, COLS), 1) < DEPTH
        beyond = (
            (outer[0], outer[2]),
            (
                jnp.where(first_half, outer[1], pltpu.roll(outer[3], DEPTH, 1)),
                jnp.where(first_half, pltpu.roll(outer[1], COLS - DEPTH, 1), outer[3]),
            ),
        )
        rows = []
        for kind in range(2):
            for ref, value in zip((left_ref, right_ref), beyond[kind]):
                rows.append(ref[pl.ds(start + kind, 1), :] + value)
            for ref in (left_ref, right_ref):
                rows.append(ref[pl.ds(start + 2 + kind, 1), :])
        stacked = jnp.concatenate([stack_rows(rows), jnp.zeros((COLS - 8, COLS), F32)], axis=0)
        turned = jnp.transpose(stacked)
        corners = pltpu.roll(turned[:8], COLS - 4, 1)
        a_ref[:MAIN, :COLS] = e2_ref[group, :, :COLS] + r_ref[:MAIN, :]
        a_ref[:MAIN, COLS:] = e2_ref[group, :, COLS:] + jnp.where(outer_lanes, turned, 0.0)
        a_ref[MAIN : MAIN + 8, :COLS] = (h2_ref[group, :, :COLS] + r_ref[MAIN : MAIN + 8, :]) * keep
        a_ref[MAIN : MAIN + 8, COLS:] = (h2_ref[group, :, COLS:] + jnp.where(outer_lanes[:8], corners, 0.0)) * keep
        f_ref[...] = dot_split(a_ref[...], z_ref[...])
        for level in range(DEPTH):
            center = f_ref[ROWS * level : ROWS * (level + 1), :]
            above = f_ref[MAIN + level : MAIN + level + 1, :]
            below = f_ref[MAIN + DEPTH + level : MAIN + DEPTH + level + 1, :]
            before = jnp.where(position == 0, above, pltpu.roll(center, 1, 0))
            after = jnp.where(position == ROWS - 1, below, pltpu.roll(center, ROWS - 1, 0))
            fine = ((2.0 * center + before) * (1.0 / 9.0), center * (1.0 / 3.0), (2.0 * center + after) * (1.0 / 9.0))
            for part in range(3):
                lanes = slice(COLS * part, COLS * (part + 1))
                for offset, value in enumerate(fine):
                    m_ref[index, part, level, pl.ds(offset, ROWS, stride=3), :] = value[:, lanes]
        if early_ref is not None:
            copies += write_group(o_ref, m_ref, group, index, sem)
    for copy in copies:
        copy.wait()


def struct(*shape):
    return jax.ShapeDtypeStruct(shape, F32)


VMEM = pl.BlockSpec(memory_space=pltpu.VMEM)
HBM = pl.BlockSpec(memory_space=pltpu.HBM)
FIELD = (GROUPS, MAIN, 2 * COLS)
RIM = (GROUPS, 8, 2 * COLS)


def call(kernel, name, ins, outs, scratch, out_specs=None):
    return pl.pallas_call(
        kernel,
        in_specs=ins,
        out_specs=out_specs or [VMEM] * len(outs),
        out_shape=outs,
        scratch_shapes=scratch,
        compiler_params=pltpu.CompilerParams(vmem_limit_bytes=VMEM_LIMIT),
        name=name,
    )


def pinned(value):
    return pltpu.with_memory_space_constraint(value, pltpu.HBM)


def edges(gradients):
    scratch = [pltpu.SemaphoreType.DMA((3,))]
    outs = [pltpu.VMEM((3, LEVELS, 3 * ROWS, COLS), F32)] + [struct(BAND, COLS)] * 2
    gradients = pinned(gradients)
    return call(edges_kernel, "edges", [HBM], outs, scratch)(gradients)


def restrict(fine, ritz_vectors):
    scratch = [
        pltpu.VMEM((2 * BLOCK, 3 * COLS), BF16),
        pltpu.VMEM((HALO, 3 * COLS), F32),
        pltpu.VMEM((COLS, COLS), F32),
        pltpu.SemaphoreType.DMA((RITZ // PIECE,)),
    ]
    outs = [pltpu.VMEM((RITZ * MAIN, COLS), F32)]
    outs += [struct(*FIELD), struct(*RIM)] + [struct(RITZ, COLS)] * 2
    outs += [pltpu.VMEM((3 * COLS, 2 * COLS), BF16)]
    flat = pinned(ritz_vectors.reshape(RITZ * MAIN, COLS))
    return call(restrict_kernel, "restrict", [VMEM, HBM], outs, scratch)(fine, flat)


def sides(*args):
    outs = [struct(SIDE, COLS)] * 2 + [struct(*FIELD), struct(*RIM)] + [struct(MAIN + 8, COLS)] * 4
    return call(sides_kernel, "sides", [VMEM] * 7, outs, [pltpu.VMEM((COLS, COLS), F32)])(*args)


def bands(*args):
    return call(bands_kernel, "bands", [VMEM] * 3, [struct(EDGE + 8, COLS)] * 2, [])(*args)


def near(held, blocks, columns):
    outs, scratch = [struct(2, RITZ)], [pltpu.VMEM((2 * COLS, COLS), F32)]
    return call(near_kernel, "near", [VMEM] * 5, outs, scratch)(held, *blocks, *columns)[0]


def far(sums, held, blocks, columns):
    outs, scratch = [struct(GROUPS, RITZ)], [pltpu.VMEM((2 * COLS, COLS), F32)]
    return call(far_kernel, "far", [VMEM] * 6, outs, scratch)(sums, held, *blocks, *columns)[0]


def update(coefficients, ritz_vectors, messages):
    outs = [pltpu.VMEM((RITZ, 2, MAIN // 2, COLS), F32), struct(GROUPS * RITZ, COLS), struct(HALO, COLS)]
    outs += [struct(BLOCK, COLS)] * 3
    scratch = [pltpu.SemaphoreType.DMA((2, RITZ // CHUNK))]
    doubled = jnp.concatenate([coefficients, coefficients], axis=0)
    return call(update_kernel, "update", [VMEM, HBM] + [VMEM] * 4, outs, scratch)(
        doubled, pinned(ritz_vectors.reshape(RITZ, 2, MAIN // 2, COLS)), *messages
    )


def own(*args):
    return call(own_kernel, "own", [VMEM] * 3, [struct(BLOCK, COLS)], [])(*args)[0]


def prolong(slots, returned, main, edge, left, right, early=None):
    scratch = [
        pltpu.VMEM((BLOCK, 2 * COLS), F32),
        pltpu.VMEM((BLOCK, 3 * COLS), F32),
        pltpu.VMEM((2 * COLS, 3 * COLS), BF16),
    ]
    stage = (2, 3, DEPTH, 3 * ROWS, COLS)
    args = (*returned, main, edge, left, right)
    specs = [VMEM] * 6
    kernel = functools.partial(prolong_kernel, slots)
    if early is None:
        return call(kernel, "prolong_early", specs, [pltpu.VMEM(stage, F32)], scratch)(*args)[0]
    scratch += [pltpu.VMEM(stage, F32), pltpu.SemaphoreType.DMA((2, 3)), pltpu.SemaphoreType.DMA((2, 3))]
    outs = [jax.ShapeDtypeStruct((GROUPS * DEPTH, 3 * ROWS, 3 * COLS), F32)]
    return call(kernel, "prolong_late", specs + [VMEM], outs, scratch, [HBM])(*args, early)[0]


def exchange_members(blocks):
    size = lax.axis_size("mem")
    order = (2, 3, 1)
    sent = {shift: lax.ppermute(blocks[shift], "mem", [(i, i ^ shift) for i in range(size)]) for shift in order}
    return [sent[shift] for shift in range(1, size)]


def exchange_sum(value, axes):
    size = lax.axis_size(axes)
    copies = jnp.broadcast_to(value[None], (size,) + value.shape)
    return jnp.sum(lax.all_to_all(copies, axes, 0, 0, tiled=True), axis=0)


def per_device(gradients, ritz_vectors, ritz_values):
    lats, lons = lax.axis_size("lat"), lax.axis_size("lon")

    gradients = gradients.reshape(gradients.shape[1:])
    fine, down, up = edges(gradients)
    over = [(i, (i + 1) % lats) for i in range(lats)]
    under = [((i + 1) % lats, i) for i in range(lats)]
    above = lax.ppermute(down, "lat", over)
    below = lax.ppermute(up, "lat", under)
    held, main, edge, first, last, weights = restrict(fine, ritz_vectors)
    to_left, to_right, main, edge, *blocks = sides(above, below, main, edge, first, last, weights)
    right = lax.ppermute(to_left, "lon", [((i + 1) % lons, i) for i in range(lons)])
    left = lax.ppermute(to_right, "lon", [(i, (i + 1) % lons) for i in range(lons)])
    spread = [blocks[0]] + exchange_members(blocks)
    near_sums = near(held, (spread[0], spread[2]), (left, right))
    left, right, near_sums, *spread = lax.optimization_barrier((left, right, near_sums, *spread))
    down, up = bands(held, left, right)
    above = lax.ppermute(down, "lat", over)
    below = lax.ppermute(up, "lat", under)
    *spread, _, _ = lax.optimization_barrier((*spread, down, up))
    partial = far(near_sums, held, (spread[3], spread[1]), (left, right))
    cells = GROUPS * DEPTH * ROWS * lats * COLS * lons
    factors = (1.0 / ritz_values - 1.0) * (1.0 / cells)
    partial, factors = lax.optimization_barrier((partial, factors))
    for shift in (1, 2):
        partial = partial + lax.ppermute(partial, "mem", [(i, i ^ shift) for i in range(4)])
    coefficients = factors[None, :] * exchange_sum(partial, ("lat", "lon"))
    messages = (above, below, left, right)
    held, weights, own_edge, *sent = update(coefficients, ritz_vectors, messages)
    returned = exchange_members([None] + sent)
    mine = own(held, weights, own_edge)
    returned = [mine] + returned
    early = prolong(EARLY, [returned[slot] for slot in EARLY], main, edge, left, right)
    output = prolong(LATE, [returned[slot] for slot in LATE], main, edge, left, right, early)
    preconditioned = output[None]
    return preconditioned, coefficients


def solution(mesh):
    placed = (P("mem", None, "lat", "lon"), P(None, "mem", "lat", "lon"), P())
    return jax.shard_map(
        per_device,
        mesh=mesh,
        in_specs=placed,
        out_specs=(P("mem", None, "lat", "lon"), P()),
        check_vma=False,
    )
```

```python
import functools

import jax
import jax.numpy as jnp
from jax import lax
from jax.experimental import pallas as pl
from jax.experimental.pallas import tpu as pltpu
from jax.sharding import PartitionSpec as P

F32 = jnp.float32
BF16 = jnp.bfloat16
RITZ = 80
GROUPS = 4
DEPTH = 4
ROWS = 32
COLS = 128
MAIN = DEPTH * ROWS
HALO = 16
BLOCK = MAIN + HALO
LEVELS = GROUPS * DEPTH
BAND = 2 * 3 * LEVELS
EDGE = DEPTH * RITZ
SIDE = RITZ + 4 * GROUPS
CHUNK = 8
PIECE = 16
KEPT = 24
EARLY = (0, 2)
LATE = (3, 1)
MIB = 1024 * 1024
VMEM_LIMIT = 24 * MIB


def member_index():
    return lax.axis_index("mem")


def has_rows():
    lat = lax.axis_index("lat")
    return [jnp.where(lat > 0, 1.0, 0.0), jnp.where(lat < lax.axis_size("lat") - 1, 1.0, 0.0)]


def iota(shape, dim):
    return lax.broadcasted_iota(jnp.int32, shape, dim)


def diagonal(rows):
    return iota((rows, COLS), 0) == iota((rows, COLS), 1)


def column_to_row(column, mask):
    spread = jnp.broadcast_to(column, mask.shape)
    return jnp.sum(jnp.where(mask, spread, 0.0), axis=0, keepdims=True)


def stack_rows(rows):
    position = iota((8, COLS), 0)
    result = jnp.zeros((8, COLS), F32)
    for index, row in enumerate(rows):
        result = jnp.where(position == index, jnp.broadcast_to(row, (8, COLS)), result)
    return result


def split(value):
    high = value.astype(BF16)
    return high, (value - high.astype(F32)).astype(BF16)


def dot_split(value, weights):
    rows = value.shape[0]
    both = jnp.dot(jnp.concatenate(split(value), axis=0), weights, preferred_element_type=F32)
    return both[:rows] + both[rows:]


def tent_weights(coarse, fine):
    tent = jnp.maximum(3 - jnp.abs(fine - 3 * coarse - 1), 0)
    left = jnp.logical_and(coarse == COLS, fine == 0)
    right = jnp.logical_and(coarse == COLS + 1, fine == 3 * COLS - 1)
    outer = jnp.where(jnp.logical_or(left, right), 1, 0)
    return jnp.where(coarse < COLS, tent, outer)


def edges_kernel(g_ref, f_ref, down_ref, up_ref, sem):
    copies = []
    for part in range(3):
        source = g_ref.at[:, :, pl.ds(COLS * part, COLS)]
        copy = pltpu.make_async_copy(source, f_ref.at[part], sem.at[part])
        copy.start()
        copies.append(copy)
    row = iota((1, 8, COLS), 1)
    plans = (
        (up_ref, 0, jnp.where(row < 4, jnp.where(row == 1, 3, jnp.where(row == 3, 1, 2)), 0), row == 0),
        (
            down_ref,
            3 * ROWS - 8,
            jnp.where(row > 3, jnp.where(row == 6, 3, jnp.where(row == 4, 1, 2)), 0),
            row == 7,
        ),
    )
    for part in range(3):
        copies[part].wait()
        for ref, start, weights, outer in plans:
            fine = f_ref[part, :, start : start + 8, :]
            place = 2 * LEVELS * part
            ref[place : place + LEVELS, :] = jnp.sum(fine * weights.astype(F32), axis=1)
            ref[place + LEVELS : place + 2 * LEVELS, :] = jnp.sum(jnp.where(outer, fine, 0.0), axis=1)


def restrict_kernel(
    f_ref, v_ref, copy_ref, e_ref, h_ref, first_ref, last_ref, w_ref, a_ref, o_ref, m_ref, sem
):
    copies = []
    for start in range(0, RITZ, PIECE):
        place = pl.ds(MAIN * start, MAIN * PIECE)
        copy = pltpu.make_async_copy(v_ref.at[place, :], copy_ref.at[place, :], sem.at[start // PIECE])
        copy.start()
        copies.append(copy)
    fine = iota((3 * COLS, 2 * COLS), 0)
    coarse = iota((3 * COLS, 2 * COLS), 1)
    w_ref[...] = tent_weights(coarse, fine).astype(F32).astype(BF16)
    position = iota((ROWS, COLS), 0)
    o_ref[...] = jnp.zeros_like(o_ref)

    def body(group, carry):
        for part in range(3):
            lanes = slice(COLS * part, COLS * (part + 1))
            for level in range(DEPTH):
                first = f_ref[part, DEPTH * group + level, pl.ds(0, ROWS, stride=3), :]
                middle = f_ref[part, DEPTH * group + level, pl.ds(1, ROWS, stride=3), :]
                third = f_ref[part, DEPTH * group + level, pl.ds(2, ROWS, stride=3), :]
                before = jnp.where(position == 0, 0.0, pltpu.roll(third, 1, 0))
                after = jnp.where(position == ROWS - 1, 0.0, pltpu.roll(first, ROWS - 1, 0))
                high, low = split(before + after + 2.0 * (first + third) + 3.0 * middle)
                start = ROWS * level
                a_ref[start : start + ROWS, lanes] = high
                a_ref[BLOCK + start : BLOCK + start + ROWS, lanes] = low
                o_ref[level : level + 1, lanes] = first[0:1]
                o_ref[DEPTH + level : DEPTH + level + 1, lanes] = third[ROWS - 1 : ROWS]
        high, low = split(o_ref[...])
        a_ref[MAIN:BLOCK, :] = high
        a_ref[BLOCK + MAIN :, :] = low
        both = jnp.dot(a_ref[...], w_ref[...], preferred_element_type=F32)
        coarse = (both[:BLOCK] + both[BLOCK:]) * (1.0 / 81.0)
        e_ref[group] = coarse[:MAIN]
        h_ref[group] = coarse[MAIN : MAIN + 8]
        return carry

    lax.fori_loop(0, GROUPS, body, 0)
    lanes = iota((MAIN, COLS), 1) // 2
    half = RITZ // 2
    for part in range(2):
        packed = jnp.zeros((MAIN, COLS), F32)
        for index in range(half):
            k = half * part + index
            if k % PIECE == 0:
                copies[k // PIECE].wait()
            turned = pltpu.roll(copy_ref[MAIN * k : MAIN * (k + 1), :], 2 * index + 1, 1)
            packed = jnp.where(lanes == index, turned, packed)
        m_ref[...] = jnp.transpose(packed)
        place = slice(half * part, half * (part + 1))
        last_ref[place, :] = m_ref[pl.ds(0, half, stride=2), :]
        first_ref[place, :] = m_ref[pl.ds(1, half, stride=2), :]


def sides_kernel(
    above_ref, below_ref, e_ref, h_ref, first_ref, last_ref, w_ref,
    left_ref, right_ref, e2_ref, h2_ref, x0_ref, x1_ref, x2_ref, x3_ref, m_ref
):
    corner = diagonal(8)
    left_ref[:RITZ, :] = first_ref[...]
    right_ref[:RITZ, :] = last_ref[...]
    position = iota((ROWS, 2 * COLS), 0)
    lanes = iota((MAIN, COLS), 1)
    packed = jnp.zeros((MAIN, COLS), F32)
    corners = ([], [])
    received = []
    for index, ref in enumerate((above_ref, below_ref)):
        parts = [has_rows()[index] * ref[2 * LEVELS * part : 2 * LEVELS * (part + 1), :] for part in range(3)]
        received.append(jnp.concatenate(parts, axis=1))
    received = dot_split(jnp.concatenate(received, axis=0), w_ref[...]) * (1.0 / 81.0)
    for group in range(GROUPS):
        place = slice(DEPTH * group, DEPTH * (group + 1))
        over, above, under, below = [received[LEVELS * i : LEVELS * (i + 1)][place] for i in range(4)]
        for level in range(DEPTH):
            rows = slice(ROWS * level, ROWS * (level + 1))
            tile = e_ref[group, rows, :]
            tile = tile + jnp.where(position == 0, above[level : level + 1, :], 0.0)
            tile = tile + jnp.where(position == ROWS - 1, below[level : level + 1, :], 0.0)
            e2_ref[group, rows, :] = tile
        edge = h_ref[group] + jnp.concatenate([over, under], axis=0)
        h2_ref[group] = edge
        for rows, lane, outer in ((corners[0], 0, COLS), (corners[1], COLS - 1, COLS + 1)):
            for source in (lane, outer):
                rows.append(column_to_row(edge[:, source : source + 1], corner))
        inner = pltpu.roll(e2_ref[group, :, :COLS], 4 * group + 1, 1)
        outer = pltpu.roll(e2_ref[group, :, COLS:], 4 * group + 2, 1)
        packed = jnp.where(lanes // 2 == 2 * group, inner, packed)
        packed = jnp.where(lanes // 2 == 2 * group + 1, outer, packed)
    m_ref[...] = jnp.transpose(packed)
    for ref, row, outer, extra in ((left_ref, 1, 2, corners[0]), (right_ref, 0, 3, corners[1])):
        for pair in range(2):
            rows = []
            for group in (2 * pair, 2 * pair + 1):
                rows.append(m_ref[4 * group + row : 4 * group + row + 1, :])
                rows.append(extra[2 * group])
                rows.append(m_ref[4 * group + outer : 4 * group + outer + 1, :])
                rows.append(extra[2 * group + 1])
            ref[RITZ + 8 * pair : RITZ + 8 * pair + 8, :] = stack_rows(rows)
    for slot, ref in enumerate((x0_ref, x1_ref, x2_ref, x3_ref)):
        group = member_index() ^ slot
        ref[:MAIN] = e2_ref[group, :, :COLS]
        ref[MAIN:] = stack_rows([m_ref[pl.ds(4 * group + 2 + side, 1), :] for side in range(2)])


def bands_kernel(v_ref, left_ref, right_ref, down_ref, up_ref):
    lanes = iota((COLS, COLS), 1)
    for ref, row in ((up_ref, 0), (down_ref, ROWS - 1)):
        corners = jnp.zeros((COLS, COLS), F32)
        for level in range(DEPTH):
            source = ROWS * level + row
            start = RITZ * level
            ref[start : start + RITZ, :] = v_ref[pl.ds(source, RITZ, stride=MAIN), :]
            for side, columns in enumerate((left_ref, right_ref)):
                target = DEPTH * side + level
                column = jnp.concatenate([columns[:RITZ, :], jnp.zeros((COLS - RITZ, COLS), F32)], axis=0)
                turned = pltpu.roll(column, (target - source) % COLS, 1)
                corners = jnp.where(lanes == target, turned, corners)
        ref[EDGE:, :] = jnp.transpose(corners)[:8]


def edge_parts(above_ref, below_ref, left_ref, right_ref):
    keep = has_rows()
    parts = []
    for index, source in enumerate((above_ref, below_ref)):
        for level in range(DEPTH):
            parts.append(keep[index] * source[RITZ * level : RITZ * (level + 1), :])
    parts += [left_ref[:RITZ, :], right_ref[:RITZ, :]]
    corners = [keep[index] * source[EDGE:, :RITZ] for index, source in enumerate((above_ref, below_ref))]
    return parts, corners


def lane_sums(v_ref, blocks, left_ref, right_ref, s_ref):
    def body(step, carry):
        base = pl.multiple_of(step * CHUNK, CHUNK)
        sums = [[jnp.zeros((8, COLS), F32) for _ in range(CHUNK)] for _ in blocks]
        for tile in range(MAIN // 8):
            fields = [block[8 * tile : 8 * tile + 8, :] for block in blocks]
            for k in range(CHUNK):
                vector = v_ref[pl.ds(pl.multiple_of((base + k) * MAIN + 8 * tile, 8), 8), :]
                for member, field in enumerate(fields):
                    sums[member][k] = sums[member][k] + vector * field
        for member, block in enumerate(blocks):
            total = stack_rows([jnp.sum(value, axis=0, keepdims=True) for value in sums[member]])
            for side, column_ref in enumerate((left_ref, right_ref)):
                total = total + column_ref[pl.ds(base, CHUNK), :] * block[MAIN + side : MAIN + side + 1, :]
            s_ref[pl.ds(COLS * member + base, CHUNK), :] = total
        return carry

    lax.fori_loop(0, RITZ // CHUNK, body, 0)
    high, low = split(s_ref[...])
    rest = (s_ref[...] - high.astype(F32) - low.astype(F32)).astype(BF16)
    ones = jnp.ones((8, 3 * COLS), BF16)
    parts = jnp.concatenate([high, low, rest], axis=1)
    sums = lax.dot_general(ones, parts, (((1,), (1,)), ((), ())), preferred_element_type=F32)
    return [sums[0:1, COLS * member : COLS * member + RITZ] for member in range(len(blocks))]


def near_kernel(v_ref, c0_ref, c2_ref, left_ref, right_ref, p_ref, s_ref):
    for index, row in enumerate(lane_sums(v_ref, (c0_ref, c2_ref), left_ref, right_ref, s_ref)):
        p_ref[index : index + 1, :] = row


def far_kernel(near_ref, v_ref, c3_ref, c1_ref, left_ref, right_ref, p_ref, s_ref):
    rows = lane_sums(v_ref, (c3_ref, c1_ref), left_ref, right_ref, s_ref)
    for slot, row in zip((0, 2, 3, 1), [near_ref[0:1, :], near_ref[1:2, :]] + rows):
        p_ref[pl.ds(member_index() ^ slot, 1), :] = row


def exact_dot(left, right, dims):
    return lax.dot_general(
        left, right, (dims, ((), ())), precision=lax.Precision.HIGHEST, preferred_element_type=F32
    )


def weighted_sums(kept_ref, rest_ref, b_ref, slots, prepare):
    half = MAIN // 2
    results = []
    for part in range(2):

        def body(index, sums, ref, first, part=part):
            if first:
                prepare(part, index)
            for offset in range(CHUNK):
                k = index * CHUNK + offset
                vector = ref[k, part]
                sums = [
                    value + b_ref[pl.ds(RITZ * member + first + k, 1), :] * vector
                    for value, member in zip(sums, slots)
                ]
            return tuple(sums)

        sums = tuple(jnp.zeros((half, COLS), F32) for _ in slots)
        sums = lax.fori_loop(0, KEPT // CHUNK, functools.partial(body, ref=kept_ref, first=0), sums)
        rest = functools.partial(body, ref=rest_ref, first=KEPT)
        results.append(lax.fori_loop(0, (RITZ - KEPT) // CHUNK, rest, sums))
    return results


def update_kernel(
    c_ref, kept_ref, v_hbm_ref, above_ref, below_ref, left_ref, right_ref,
    v_ref, b_ref, edge_ref, u1_ref, u2_ref, u3_ref, sem
):
    me = member_index()
    outs = (None, u1_ref, u2_ref, u3_ref)
    pieces = (RITZ - KEPT) // CHUNK

    def copy(part, piece):
        source = v_hbm_ref.at[pl.ds(KEPT + piece * CHUNK, CHUNK), part]
        return pltpu.make_async_copy(source, v_ref.at[pl.ds(piece * CHUNK, CHUNK), part], sem.at[part, piece])

    for part in range(2):
        for piece in range(pieces):
            copy(part, piece).start()
    coefficients = c_ref[...]
    places = [iota((8, COLS), 0) == (me ^ member) for member in range(GROUPS)]
    chosen = jnp.concatenate([jnp.where(place, 1.0, 0.0) for place in places], axis=1)
    spread = exact_dot(coefficients, chosen, ((0,), (0,)))
    for member in range(GROUPS):
        b_ref[RITZ * member : RITZ * (member + 1), :] = spread[:, COLS * member : COLS * (member + 1)]
    swap = jnp.where(iota((8, 8), 1) == (me ^ iota((8, 8), 0)), 1.0, 0.0)
    ordered = exact_dot(swap, coefficients, ((1,), (0,)))
    parts, corners = edge_parts(above_ref, below_ref, left_ref, right_ref)
    edge = exact_dot(ordered, jnp.concatenate(parts, axis=1), ((1,), (0,)))
    corners = [exact_dot(ordered, corner, ((1,), (1,))) for corner in corners]
    places = list(range(2 * DEPTH)) + [8, 10]
    for member in range(GROUPS):
        ref, start = (outs[member], MAIN) if member else (edge_ref, 0)
        ref[start + 8 : start + HALO, :] = jnp.zeros((HALO - 8, COLS), F32)
        for index, place in enumerate(places):
            row = edge[member : member + 1, COLS * index : COLS * (index + 1)]
            ref[start + place : start + place + 1, :] = row
        for index, place in enumerate((9, 11)):
            ref[start + place : start + place + 1, :8] = corners[index][member : member + 1, :]

    def prepare(part, index):
        copy(part, index).wait()

    half = MAIN // 2
    for part, sums in enumerate(weighted_sums(kept_ref, v_ref, b_ref, (1, 2, 3), prepare)):
        for member, value in zip((1, 2, 3), sums):
            outs[member][half * part : half * (part + 1), :] = value


def keep_kernel(v_ref, kept_ref, sem):
    copy = pltpu.make_async_copy(v_ref.at[pl.ds(0, KEPT)], kept_ref, sem.at[0])
    copy.start()
    copy.wait()


def own_kernel(kept_ref, v_ref, b_ref, edge_ref, u0_ref):
    half = MAIN // 2
    for part, sums in enumerate(weighted_sums(kept_ref, v_ref, b_ref, (0,), lambda part, index: None)):
        u0_ref[half * part : half * (part + 1), :] = sums[0]
    u0_ref[MAIN:, :] = edge_ref[...]


def write_group(o_ref, m_ref, group, index, sem):
    copies = []
    for part in range(3):
        target = o_ref.at[pl.ds(DEPTH * group, DEPTH), :, pl.ds(COLS * part, COLS)]
        copy = pltpu.make_async_copy(m_ref.at[index, part], target, sem.at[index, part])
        copy.start()
        copies.append(copy)
    return copies


def prolong_kernel(slots, ra_ref, rb_ref, e2_ref, h2_ref, left_ref, right_ref, *refs):
    early_ref = None
    copies = []
    if len(refs) == 4:
        m_ref, a_ref, f_ref, z_ref = refs
    else:
        early_ref, o_ref, a_ref, f_ref, z_ref, m_ref, early_sem, sem = refs
        for index, slot in enumerate(EARLY):
            copies += write_group(o_ref, early_ref, member_index() ^ slot, index, early_sem)
    coarse = iota((2 * COLS, 3 * COLS), 0)
    fine = iota((2 * COLS, 3 * COLS), 1)
    coarse = jnp.where(coarse == COLS + 2, 0, jnp.where(coarse == COLS + 3, COLS - 1, coarse))
    a_ref[MAIN + 8 :, :] = jnp.zeros((BLOCK - MAIN - 8, 2 * COLS), F32)
    z_ref[...] = tent_weights(coarse, fine).astype(F32).astype(BF16)
    row = iota((8, COLS), 0)
    keep = jnp.where(row < DEPTH, *has_rows())
    outer_lanes = iota((MAIN, COLS), 1) < 4
    position = iota((ROWS, 3 * COLS), 0)
    for index, (slot, r_ref) in enumerate(zip(slots, (ra_ref, rb_ref))):
        group = member_index() ^ slot
        start = RITZ + 4 * group
        outer = [r_ref[MAIN + 8 + kind : MAIN + 9 + kind, :] for kind in range(4)]
        first_half = iota((1, COLS), 1) < DEPTH
        beyond = (
            (outer[0], outer[2]),
            (
                jnp.where(first_half, outer[1], pltpu.roll(outer[3], DEPTH, 1)),
                jnp.where(first_half, pltpu.roll(outer[1], COLS - DEPTH, 1), outer[3]),
            ),
        )
        rows = []
        for kind in range(2):
            for ref, value in zip((left_ref, right_ref), beyond[kind]):
                rows.append(ref[pl.ds(start + kind, 1), :] + value)
            for ref in (left_ref, right_ref):
                rows.append(ref[pl.ds(start + 2 + kind, 1), :])
        stacked = jnp.concatenate([stack_rows(rows), jnp.zeros((COLS - 8, COLS), F32)], axis=0)
        turned = jnp.transpose(stacked)
        corners = pltpu.roll(turned[:8], COLS - 4, 1)
        a_ref[:MAIN, :COLS] = e2_ref[group, :, :COLS] + r_ref[:MAIN, :]
        a_ref[:MAIN, COLS:] = e2_ref[group, :, COLS:] + jnp.where(outer_lanes, turned, 0.0)
        a_ref[MAIN : MAIN + 8, :COLS] = (h2_ref[group, :, :COLS] + r_ref[MAIN : MAIN + 8, :]) * keep
        a_ref[MAIN : MAIN + 8, COLS:] = (h2_ref[group, :, COLS:] + jnp.where(outer_lanes[:8], corners, 0.0)) * keep
        f_ref[...] = dot_split(a_ref[...], z_ref[...])
        for level in range(DEPTH):
            center = f_ref[ROWS * level : ROWS * (level + 1), :]
            above = f_ref[MAIN + level : MAIN + level + 1, :]
            below = f_ref[MAIN + DEPTH + level : MAIN + DEPTH + level + 1, :]
            before = jnp.where(position == 0, above, pltpu.roll(center, 1, 0))
            after = jnp.where(position == ROWS - 1, below, pltpu.roll(center, ROWS - 1, 0))
            fine = ((2.0 * center + before) * (1.0 / 9.0), center * (1.0 / 3.0), (2.0 * center + after) * (1.0 / 9.0))
            for part in range(3):
                lanes = slice(COLS * part, COLS * (part + 1))
                for offset, value in enumerate(fine):
                    m_ref[index, part, level, pl.ds(offset, ROWS, stride=3), :] = value[:, lanes]
        if early_ref is not None:
            copies += write_group(o_ref, m_ref, group, index, sem)
    for copy in copies:
        copy.wait()


def struct(*shape):
    return jax.ShapeDtypeStruct(shape, F32)


VMEM = pl.BlockSpec(memory_space=pltpu.VMEM)
HBM = pl.BlockSpec(memory_space=pltpu.HBM)
FIELD = (GROUPS, MAIN, 2 * COLS)
RIM = (GROUPS, 8, 2 * COLS)


def call(kernel, name, ins, outs, scratch, out_specs=None):
    return pl.pallas_call(
        kernel,
        in_specs=ins,
        out_specs=out_specs or [VMEM] * len(outs),
        out_shape=outs,
        scratch_shapes=scratch,
        compiler_params=pltpu.CompilerParams(vmem_limit_bytes=VMEM_LIMIT),
        name=name,
    )


def pinned(value):
    return pltpu.with_memory_space_constraint(value, pltpu.HBM)


def edges(gradients):
    scratch = [pltpu.SemaphoreType.DMA((3,))]
    outs = [pltpu.VMEM((3, LEVELS, 3 * ROWS, COLS), F32)] + [struct(BAND, COLS)] * 2
    gradients = pinned(gradients)
    return call(edges_kernel, "edges", [HBM], outs, scratch)(gradients)


def restrict(fine, ritz_vectors):
    scratch = [
        pltpu.VMEM((2 * BLOCK, 3 * COLS), BF16),
        pltpu.VMEM((HALO, 3 * COLS), F32),
        pltpu.VMEM((COLS, COLS), F32),
        pltpu.SemaphoreType.DMA((RITZ // PIECE,)),
    ]
    outs = [pltpu.VMEM((RITZ * MAIN, COLS), F32)]
    outs += [struct(*FIELD), struct(*RIM)] + [struct(RITZ, COLS)] * 2
    outs += [pltpu.VMEM((3 * COLS, 2 * COLS), BF16)]
    flat = pinned(ritz_vectors.reshape(RITZ * MAIN, COLS))
    return call(restrict_kernel, "restrict", [VMEM, HBM], outs, scratch)(fine, flat)


def sides(*args):
    outs = [struct(SIDE, COLS)] * 2 + [struct(*FIELD), struct(*RIM)] + [struct(MAIN + 8, COLS)] * 4
    return call(sides_kernel, "sides", [VMEM] * 7, outs, [pltpu.VMEM((COLS, COLS), F32)])(*args)


def bands(*args):
    return call(bands_kernel, "bands", [VMEM] * 3, [struct(EDGE + 8, COLS)] * 2, [])(*args)


def near(held, blocks, columns):
    outs, scratch = [struct(2, RITZ)], [pltpu.VMEM((2 * COLS, COLS), F32)]
    return call(near_kernel, "near", [VMEM] * 5, outs, scratch)(held, *blocks, *columns)[0]


def far(sums, held, blocks, columns):
    outs, scratch = [struct(GROUPS, RITZ)], [pltpu.VMEM((2 * COLS, COLS), F32)]
    return call(far_kernel, "far", [VMEM] * 6, outs, scratch)(sums, held, *blocks, *columns)[0]


def update(coefficients, kept, ritz_vectors, messages):
    outs = [pltpu.VMEM((RITZ - KEPT, 2, MAIN // 2, COLS), F32), struct(GROUPS * RITZ, COLS), struct(HALO, COLS)]
    outs += [struct(BLOCK, COLS)] * 3
    scratch = [pltpu.SemaphoreType.DMA((2, (RITZ - KEPT) // CHUNK))]
    doubled = jnp.concatenate([coefficients, coefficients], axis=0)
    return call(update_kernel, "update", [VMEM, VMEM, HBM] + [VMEM] * 4, outs, scratch)(
        doubled, kept, pinned(ritz_vectors.reshape(RITZ, 2, MAIN // 2, COLS)), *messages
    )


def keep(ritz_vectors):
    outs = [pltpu.VMEM((KEPT, 2, MAIN // 2, COLS), F32)]
    tiles = pinned(ritz_vectors.reshape(RITZ, 2, MAIN // 2, COLS))
    return call(keep_kernel, "keep", [HBM], outs, [pltpu.SemaphoreType.DMA((1,))])(tiles)[0]


def own(*args):
    return call(own_kernel, "own", [VMEM] * 4, [struct(BLOCK, COLS)], [])(*args)[0]


def prolong(slots, returned, main, edge, left, right, early=None):
    scratch = [
        pltpu.VMEM((BLOCK, 2 * COLS), F32),
        pltpu.VMEM((BLOCK, 3 * COLS), F32),
        pltpu.VMEM((2 * COLS, 3 * COLS), BF16),
    ]
    stage = (2, 3, DEPTH, 3 * ROWS, COLS)
    args = (*returned, main, edge, left, right)
    specs = [VMEM] * 6
    kernel = functools.partial(prolong_kernel, slots)
    if early is None:
        return call(kernel, "prolong_early", specs, [pltpu.VMEM(stage, F32)], scratch)(*args)[0]
    scratch += [pltpu.VMEM(stage, F32), pltpu.SemaphoreType.DMA((2, 3)), pltpu.SemaphoreType.DMA((2, 3))]
    outs = [jax.ShapeDtypeStruct((GROUPS * DEPTH, 3 * ROWS, 3 * COLS), F32)]
    return call(kernel, "prolong_late", specs + [VMEM], outs, scratch, [HBM])(*args, early)[0]


def exchange_members(blocks):
    size = lax.axis_size("mem")
    order = (2, 3, 1)
    sent = {shift: lax.ppermute(blocks[shift], "mem", [(i, i ^ shift) for i in range(size)]) for shift in order}
    return [sent[shift] for shift in range(1, size)]


def exchange_sum(value, axes):
    size = lax.axis_size(axes)
    copies = jnp.broadcast_to(value[None], (size,) + value.shape)
    return jnp.sum(lax.all_to_all(copies, axes, 0, 0, tiled=True), axis=0)


def per_device(gradients, ritz_vectors, ritz_values):
    lats, lons = lax.axis_size("lat"), lax.axis_size("lon")

    gradients = gradients.reshape(gradients.shape[1:])
    fine, down, up = edges(gradients)
    over = [(i, (i + 1) % lats) for i in range(lats)]
    under = [((i + 1) % lats, i) for i in range(lats)]
    above = lax.ppermute(down, "lat", over)
    below = lax.ppermute(up, "lat", under)
    held, main, edge, first, last, weights = restrict(fine, ritz_vectors)
    to_left, to_right, main, edge, *blocks = sides(above, below, main, edge, first, last, weights)
    right = lax.ppermute(to_left, "lon", [((i + 1) % lons, i) for i in range(lons)])
    left = lax.ppermute(to_right, "lon", [(i, (i + 1) % lons) for i in range(lons)])
    spread = [blocks[0]] + exchange_members(blocks)
    near_sums = near(held, (spread[0], spread[2]), (left, right))
    left, right, near_sums, *spread = lax.optimization_barrier((left, right, near_sums, *spread))
    down, up = bands(held, left, right)
    above = lax.ppermute(down, "lat", over)
    below = lax.ppermute(up, "lat", under)
    *spread, _, _ = lax.optimization_barrier((*spread, down, up))
    partial = far(near_sums, held, (spread[3], spread[1]), (left, right))
    cells = GROUPS * DEPTH * ROWS * lats * COLS * lons
    factors = (1.0 / ritz_values - 1.0) * (1.0 / cells)
    partial, factors, stored = lax.optimization_barrier((partial, factors, ritz_vectors))
    kept = keep(stored)
    for shift in (1, 2):
        partial = partial + lax.ppermute(partial, "mem", [(i, i ^ shift) for i in range(4)])
    coefficients = factors[None, :] * exchange_sum(partial, ("lat", "lon"))
    messages = (above, below, left, right)
    held, weights, own_edge, *sent = update(coefficients, kept, ritz_vectors, messages)
    returned = exchange_members([None] + sent)
    mine = own(kept, held, weights, own_edge)
    returned = [mine] + returned
    early = prolong(EARLY, [returned[slot] for slot in EARLY], main, edge, left, right)
    output = prolong(LATE, [returned[slot] for slot in LATE], main, edge, left, right, early)
    preconditioned = output[None]
    return preconditioned, coefficients


def solution(mesh):
    placed = (P("mem", None, "lat", "lon"), P(None, "mem", "lat", "lon"), P())
    return jax.shard_map(
        per_device,
        mesh=mesh,
        in_specs=placed,
        out_specs=(P("mem", None, "lat", "lon"), P()),
        check_vma=False,
    )
```

```python
import functools

import jax
import jax.numpy as jnp
from jax import lax
from jax.experimental import pallas as pl
from jax.experimental.pallas import tpu as pltpu
from jax.sharding import PartitionSpec as P

F32 = jnp.float32
BF16 = jnp.bfloat16
RITZ = 80
GROUPS = 4
DEPTH = 4
ROWS = 32
COLS = 128
MAIN = DEPTH * ROWS
HALO = 16
BLOCK = MAIN + HALO
LEVELS = GROUPS * DEPTH
BAND = 2 * 3 * LEVELS
EDGE = DEPTH * RITZ
SIDE = RITZ + 4 * GROUPS
CHUNK = 8
PIECE = 8
EARLY = (0, 2)
LATE = (3, 1)
MIB = 1024 * 1024
VMEM_LIMIT = 24 * MIB


def member_index():
    return lax.axis_index("mem")


def has_rows():
    lat = lax.axis_index("lat")
    return [jnp.where(lat > 0, 1.0, 0.0), jnp.where(lat < lax.axis_size("lat") - 1, 1.0, 0.0)]


def iota(shape, dim):
    return lax.broadcasted_iota(jnp.int32, shape, dim)


def diagonal(rows):
    return iota((rows, COLS), 0) == iota((rows, COLS), 1)


def column_to_row(column, mask):
    spread = jnp.broadcast_to(column, mask.shape)
    return jnp.sum(jnp.where(mask, spread, 0.0), axis=0, keepdims=True)


def stack_rows(rows):
    position = iota((8, COLS), 0)
    result = jnp.zeros((8, COLS), F32)
    for index, row in enumerate(rows):
        result = jnp.where(position == index, jnp.broadcast_to(row, (8, COLS)), result)
    return result


def split(value):
    high = value.astype(BF16)
    return high, (value - high.astype(F32)).astype(BF16)


def dot_split(value, weights):
    rows = value.shape[0]
    both = jnp.dot(jnp.concatenate(split(value), axis=0), weights, preferred_element_type=F32)
    return both[:rows] + both[rows:]


def tent_weights(coarse, fine):
    tent = jnp.maximum(3 - jnp.abs(fine - 3 * coarse - 1), 0)
    left = jnp.logical_and(coarse == COLS, fine == 0)
    right = jnp.logical_and(coarse == COLS + 1, fine == 3 * COLS - 1)
    outer = jnp.where(jnp.logical_or(left, right), 1, 0)
    return jnp.where(coarse < COLS, tent, outer)


def edges_kernel(g_ref, f_ref, down_ref, up_ref, sem):
    copies = []
    for part in range(3):
        source = g_ref.at[:, :, pl.ds(COLS * part, COLS)]
        copy = pltpu.make_async_copy(source, f_ref.at[part], sem.at[part])
        copy.start()
        copies.append(copy)
    row = iota((1, 8, COLS), 1)
    plans = (
        (up_ref, 0, jnp.where(row < 4, jnp.where(row == 1, 3, jnp.where(row == 3, 1, 2)), 0), row == 0),
        (
            down_ref,
            3 * ROWS - 8,
            jnp.where(row > 3, jnp.where(row == 6, 3, jnp.where(row == 4, 1, 2)), 0),
            row == 7,
        ),
    )
    for part in range(3):
        copies[part].wait()
        for ref, start, weights, outer in plans:
            fine = f_ref[part, :, start : start + 8, :]
            place = 2 * LEVELS * part
            ref[place : place + LEVELS, :] = jnp.sum(fine * weights.astype(F32), axis=1)
            ref[place + LEVELS : place + 2 * LEVELS, :] = jnp.sum(jnp.where(outer, fine, 0.0), axis=1)


def restrict_kernel(
    f_ref, v_ref, copy_ref, e_ref, h_ref, first_ref, last_ref, w_ref, a_ref, o_ref, m_ref, sem
):
    copies = []
    for start in range(0, RITZ, PIECE):
        place = pl.ds(MAIN * start, MAIN * PIECE)
        copy = pltpu.make_async_copy(v_ref.at[place, :], copy_ref.at[place, :], sem.at[start // PIECE])
        copy.start()
        copies.append(copy)
    fine = iota((3 * COLS, 2 * COLS), 0)
    coarse = iota((3 * COLS, 2 * COLS), 1)
    w_ref[...] = tent_weights(coarse, fine).astype(F32).astype(BF16)
    position = iota((ROWS, COLS), 0)
    o_ref[...] = jnp.zeros_like(o_ref)

    def body(group, carry):
        for part in range(3):
            lanes = slice(COLS * part, COLS * (part + 1))
            for level in range(DEPTH):
                first = f_ref[part, DEPTH * group + level, pl.ds(0, ROWS, stride=3), :]
                middle = f_ref[part, DEPTH * group + level, pl.ds(1, ROWS, stride=3), :]
                third = f_ref[part, DEPTH * group + level, pl.ds(2, ROWS, stride=3), :]
                before = jnp.where(position == 0, 0.0, pltpu.roll(third, 1, 0))
                after = jnp.where(position == ROWS - 1, 0.0, pltpu.roll(first, ROWS - 1, 0))
                high, low = split(before + after + 2.0 * (first + third) + 3.0 * middle)
                start = ROWS * level
                a_ref[start : start + ROWS, lanes] = high
                a_ref[BLOCK + start : BLOCK + start + ROWS, lanes] = low
                o_ref[level : level + 1, lanes] = first[0:1]
                o_ref[DEPTH + level : DEPTH + level + 1, lanes] = third[ROWS - 1 : ROWS]
        high, low = split(o_ref[...])
        a_ref[MAIN:BLOCK, :] = high
        a_ref[BLOCK + MAIN :, :] = low
        both = jnp.dot(a_ref[...], w_ref[...], preferred_element_type=F32)
        coarse = (both[:BLOCK] + both[BLOCK:]) * (1.0 / 81.0)
        e_ref[group] = coarse[:MAIN]
        h_ref[group] = coarse[MAIN : MAIN + 8]
        return carry

    lax.fori_loop(0, GROUPS, body, 0)
    lanes = iota((MAIN, COLS), 1) // 2
    half = RITZ // 2
    for part in range(2):
        packed = jnp.zeros((MAIN, COLS), F32)
        for index in range(half):
            k = half * part + index
            if k % PIECE == 0:
                copies[k // PIECE].wait()
            turned = pltpu.roll(copy_ref[MAIN * k : MAIN * (k + 1), :], 2 * index + 1, 1)
            packed = jnp.where(lanes == index, turned, packed)
        m_ref[...] = jnp.transpose(packed)
        place = slice(half * part, half * (part + 1))
        last_ref[place, :] = m_ref[pl.ds(0, half, stride=2), :]
        first_ref[place, :] = m_ref[pl.ds(1, half, stride=2), :]


def sides_kernel(
    above_ref, below_ref, e_ref, h_ref, first_ref, last_ref, w_ref,
    left_ref, right_ref, e2_ref, h2_ref, x0_ref, x1_ref, x2_ref, x3_ref, m_ref
):
    corner = diagonal(8)
    left_ref[:RITZ, :] = first_ref[...]
    right_ref[:RITZ, :] = last_ref[...]
    position = iota((ROWS, 2 * COLS), 0)
    lanes = iota((MAIN, COLS), 1)
    packed = jnp.zeros((MAIN, COLS), F32)
    corners = ([], [])
    received = []
    for index, ref in enumerate((above_ref, below_ref)):
        parts = [has_rows()[index] * ref[2 * LEVELS * part : 2 * LEVELS * (part + 1), :] for part in range(3)]
        received.append(jnp.concatenate(parts, axis=1))
    received = dot_split(jnp.concatenate(received, axis=0), w_ref[...]) * (1.0 / 81.0)
    for group in range(GROUPS):
        place = slice(DEPTH * group, DEPTH * (group + 1))
        over, above, under, below = [received[LEVELS * i : LEVELS * (i + 1)][place] for i in range(4)]
        for level in range(DEPTH):
            rows = slice(ROWS * level, ROWS * (level + 1))
            tile = e_ref[group, rows, :]
            tile = tile + jnp.where(position == 0, above[level : level + 1, :], 0.0)
            tile = tile + jnp.where(position == ROWS - 1, below[level : level + 1, :], 0.0)
            e2_ref[group, rows, :] = tile
        edge = h_ref[group] + jnp.concatenate([over, under], axis=0)
        h2_ref[group] = edge
        for rows, lane, outer in ((corners[0], 0, COLS), (corners[1], COLS - 1, COLS + 1)):
            for source in (lane, outer):
                rows.append(column_to_row(edge[:, source : source + 1], corner))
        inner = pltpu.roll(e2_ref[group, :, :COLS], 4 * group + 1, 1)
        outer = pltpu.roll(e2_ref[group, :, COLS:], 4 * group + 2, 1)
        packed = jnp.where(lanes // 2 == 2 * group, inner, packed)
        packed = jnp.where(lanes // 2 == 2 * group + 1, outer, packed)
    m_ref[...] = jnp.transpose(packed)
    for ref, row, outer, extra in ((left_ref, 1, 2, corners[0]), (right_ref, 0, 3, corners[1])):
        for pair in range(2):
            rows = []
            for group in (2 * pair, 2 * pair + 1):
                rows.append(m_ref[4 * group + row : 4 * group + row + 1, :])
                rows.append(extra[2 * group])
                rows.append(m_ref[4 * group + outer : 4 * group + outer + 1, :])
                rows.append(extra[2 * group + 1])
            ref[RITZ + 8 * pair : RITZ + 8 * pair + 8, :] = stack_rows(rows)
    for slot, ref in enumerate((x0_ref, x1_ref, x2_ref, x3_ref)):
        group = member_index() ^ slot
        ref[:MAIN] = e2_ref[group, :, :COLS]
        ref[MAIN:] = stack_rows([m_ref[pl.ds(4 * group + 2 + side, 1), :] for side in range(2)])


def bands_kernel(v_ref, left_ref, right_ref, down_ref, up_ref):
    lanes = iota((COLS, COLS), 1)
    for ref, row in ((up_ref, 0), (down_ref, ROWS - 1)):
        corners = jnp.zeros((COLS, COLS), F32)
        for level in range(DEPTH):
            source = ROWS * level + row
            start = RITZ * level
            ref[start : start + RITZ, :] = v_ref[pl.ds(source, RITZ, stride=MAIN), :]
            for side, columns in enumerate((left_ref, right_ref)):
                target = DEPTH * side + level
                column = jnp.concatenate([columns[:RITZ, :], jnp.zeros((COLS - RITZ, COLS), F32)], axis=0)
                turned = pltpu.roll(column, (target - source) % COLS, 1)
                corners = jnp.where(lanes == target, turned, corners)
        ref[EDGE:, :] = jnp.transpose(corners)[:8]


def edge_parts(above_ref, below_ref, left_ref, right_ref):
    keep = has_rows()
    parts = []
    for index, source in enumerate((above_ref, below_ref)):
        for level in range(DEPTH):
            parts.append(keep[index] * source[RITZ * level : RITZ * (level + 1), :])
    parts += [left_ref[:RITZ, :], right_ref[:RITZ, :]]
    corners = [keep[index] * source[EDGE:, :RITZ] for index, source in enumerate((above_ref, below_ref))]
    return parts, corners


def lane_sums(v_ref, blocks, left_ref, right_ref, s_ref):
    def body(step, carry):
        base = pl.multiple_of(step * CHUNK, CHUNK)
        sums = [[jnp.zeros((8, COLS), F32) for _ in range(CHUNK)] for _ in blocks]
        for tile in range(MAIN // 8):
            fields = [block[8 * tile : 8 * tile + 8, :] for block in blocks]
            for k in range(CHUNK):
                vector = v_ref[pl.ds(pl.multiple_of((base + k) * MAIN + 8 * tile, 8), 8), :]
                for member, field in enumerate(fields):
                    sums[member][k] = sums[member][k] + vector * field
        for member, block in enumerate(blocks):
            total = stack_rows([jnp.sum(value, axis=0, keepdims=True) for value in sums[member]])
            for side, column_ref in enumerate((left_ref, right_ref)):
                total = total + column_ref[pl.ds(base, CHUNK), :] * block[MAIN + side : MAIN + side + 1, :]
            s_ref[pl.ds(COLS * member + base, CHUNK), :] = total
        return carry

    lax.fori_loop(0, RITZ // CHUNK, body, 0)
    high, low = split(s_ref[...])
    rest = (s_ref[...] - high.astype(F32) - low.astype(F32)).astype(BF16)
    ones = jnp.ones((8, 3 * COLS), BF16)
    parts = jnp.concatenate([high, low, rest], axis=1)
    sums = lax.dot_general(ones, parts, (((1,), (1,)), ((), ())), preferred_element_type=F32)
    return [sums[0:1, COLS * member : COLS * member + RITZ] for member in range(len(blocks))]


def near_kernel(v_ref, c0_ref, c2_ref, left_ref, right_ref, p_ref, s_ref):
    for index, row in enumerate(lane_sums(v_ref, (c0_ref, c2_ref), left_ref, right_ref, s_ref)):
        p_ref[index : index + 1, :] = row


def far_kernel(near_ref, v_ref, c3_ref, c1_ref, left_ref, right_ref, p_ref, s_ref):
    rows = lane_sums(v_ref, (c3_ref, c1_ref), left_ref, right_ref, s_ref)
    for slot, row in zip((0, 2, 3, 1), [near_ref[0:1, :], near_ref[1:2, :]] + rows):
        p_ref[pl.ds(member_index() ^ slot, 1), :] = row


def exact_dot(left, right, dims):
    return lax.dot_general(
        left, right, (dims, ((), ())), precision=lax.Precision.HIGHEST, preferred_element_type=F32
    )


def weighted_sums(v_ref, b_ref, slots, prepare):
    half = MAIN // 2
    results = []
    for part in range(2):

        def body(index, sums, part=part):
            prepare(part, index)
            for offset in range(CHUNK):
                k = index * CHUNK + offset
                vector = v_ref[k, part]
                sums = [
                    value + b_ref[pl.ds(RITZ * member + k, 1), :] * vector for value, member in zip(sums, slots)
                ]
            return tuple(sums)

        zeros = tuple(jnp.zeros((half, COLS), F32) for _ in slots)
        results.append(lax.fori_loop(0, RITZ // CHUNK, body, zeros))
    return results


def update_kernel(
    c_ref, v_hbm_ref, above_ref, below_ref, left_ref, right_ref,
    v_ref, b_ref, edge_ref, u1_ref, u2_ref, u3_ref, sem
):
    me = member_index()
    outs = (None, u1_ref, u2_ref, u3_ref)
    pieces = RITZ // CHUNK

    def copy(part, piece):
        source = v_hbm_ref.at[pl.ds(piece * CHUNK, CHUNK), part]
        return pltpu.make_async_copy(source, v_ref.at[pl.ds(piece * CHUNK, CHUNK), part], sem.at[part, piece])

    for part in range(2):
        for piece in range(pieces):
            copy(part, piece).start()
    coefficients = c_ref[...]
    places = [iota((8, COLS), 0) == (me ^ member) for member in range(GROUPS)]
    chosen = jnp.concatenate([jnp.where(place, 1.0, 0.0) for place in places], axis=1)
    spread = exact_dot(coefficients, chosen, ((0,), (0,)))
    for member in range(GROUPS):
        b_ref[RITZ * member : RITZ * (member + 1), :] = spread[:, COLS * member : COLS * (member + 1)]
    swap = jnp.where(iota((8, 8), 1) == (me ^ iota((8, 8), 0)), 1.0, 0.0)
    ordered = exact_dot(swap, coefficients, ((1,), (0,)))
    parts, corners = edge_parts(above_ref, below_ref, left_ref, right_ref)
    edge = exact_dot(ordered, jnp.concatenate(parts, axis=1), ((1,), (0,)))
    corners = [exact_dot(ordered, corner, ((1,), (1,))) for corner in corners]
    places = list(range(2 * DEPTH)) + [8, 10]
    for member in range(GROUPS):
        ref, start = (outs[member], MAIN) if member else (edge_ref, 0)
        ref[start + 8 : start + HALO, :] = jnp.zeros((HALO - 8, COLS), F32)
        for index, place in enumerate(places):
            row = edge[member : member + 1, COLS * index : COLS * (index + 1)]
            ref[start + place : start + place + 1, :] = row
        for index, place in enumerate((9, 11)):
            ref[start + place : start + place + 1, :8] = corners[index][member : member + 1, :]

    def prepare(part, index):
        copy(part, index).wait()

    half = MAIN // 2
    for part, sums in enumerate(weighted_sums(v_ref, b_ref, (1, 2, 3), prepare)):
        for member, value in zip((1, 2, 3), sums):
            outs[member][half * part : half * (part + 1), :] = value


def own_kernel(v_ref, b_ref, edge_ref, u0_ref):
    half = MAIN // 2
    for part, sums in enumerate(weighted_sums(v_ref, b_ref, (0,), lambda part, index: None)):
        u0_ref[half * part : half * (part + 1), :] = sums[0]
    u0_ref[MAIN:, :] = edge_ref[...]


def write_group(o_ref, m_ref, group, index, sem):
    copies = []
    for part in range(3):
        target = o_ref.at[pl.ds(DEPTH * group, DEPTH), :, pl.ds(COLS * part, COLS)]
        copy = pltpu.make_async_copy(m_ref.at[index, part], target, sem.at[index, part])
        copy.start()
        copies.append(copy)
    return copies


def prolong_kernel(slots, ra_ref, rb_ref, e2_ref, h2_ref, left_ref, right_ref, *refs):
    early_ref = None
    copies = []
    if len(refs) == 4:
        m_ref, a_ref, f_ref, z_ref = refs
    else:
        early_ref, o_ref, a_ref, f_ref, z_ref, m_ref, early_sem, sem = refs
        for index, slot in enumerate(EARLY):
            copies += write_group(o_ref, early_ref, member_index() ^ slot, index, early_sem)
    coarse = iota((2 * COLS, 3 * COLS), 0)
    fine = iota((2 * COLS, 3 * COLS), 1)
    coarse = jnp.where(coarse == COLS + 2, 0, jnp.where(coarse == COLS + 3, COLS - 1, coarse))
    a_ref[MAIN + 8 :, :] = jnp.zeros((BLOCK - MAIN - 8, 2 * COLS), F32)
    z_ref[...] = tent_weights(coarse, fine).astype(F32).astype(BF16)
    row = iota((8, COLS), 0)
    keep = jnp.where(row < DEPTH, *has_rows())
    outer_lanes = iota((MAIN, COLS), 1) < 4
    position = iota((ROWS, 3 * COLS), 0)
    for index, (slot, r_ref) in enumerate(zip(slots, (ra_ref, rb_ref))):
        group = member_index() ^ slot
        start = RITZ + 4 * group
        outer = [r_ref[MAIN + 8 + kind : MAIN + 9 + kind, :] for kind in range(4)]
        first_half = iota((1, COLS), 1) < DEPTH
        beyond = (
            (outer[0], outer[2]),
            (
                jnp.where(first_half, outer[1], pltpu.roll(outer[3], DEPTH, 1)),
                jnp.where(first_half, pltpu.roll(outer[1], COLS - DEPTH, 1), outer[3]),
            ),
        )
        rows = []
        for kind in range(2):
            for ref, value in zip((left_ref, right_ref), beyond[kind]):
                rows.append(ref[pl.ds(start + kind, 1), :] + value)
            for ref in (left_ref, right_ref):
                rows.append(ref[pl.ds(start + 2 + kind, 1), :])
        stacked = jnp.concatenate([stack_rows(rows), jnp.zeros((COLS - 8, COLS), F32)], axis=0)
        turned = jnp.transpose(stacked)
        corners = pltpu.roll(turned[:8], COLS - 4, 1)
        a_ref[:MAIN, :COLS] = e2_ref[group, :, :COLS] + r_ref[:MAIN, :]
        a_ref[:MAIN, COLS:] = e2_ref[group, :, COLS:] + jnp.where(outer_lanes, turned, 0.0)
        a_ref[MAIN : MAIN + 8, :COLS] = (h2_ref[group, :, :COLS] + r_ref[MAIN : MAIN + 8, :]) * keep
        a_ref[MAIN : MAIN + 8, COLS:] = (h2_ref[group, :, COLS:] + jnp.where(outer_lanes[:8], corners, 0.0)) * keep
        f_ref[...] = dot_split(a_ref[...], z_ref[...])
        for level in range(DEPTH):
            center = f_ref[ROWS * level : ROWS * (level + 1), :]
            above = f_ref[MAIN + level : MAIN + level + 1, :]
            below = f_ref[MAIN + DEPTH + level : MAIN + DEPTH + level + 1, :]
            before = jnp.where(position == 0, above, pltpu.roll(center, 1, 0))
            after = jnp.where(position == ROWS - 1, below, pltpu.roll(center, ROWS - 1, 0))
            fine = ((2.0 * center + before) * (1.0 / 9.0), center * (1.0 / 3.0), (2.0 * center + after) * (1.0 / 9.0))
            for part in range(3):
                lanes = slice(COLS * part, COLS * (part + 1))
                for offset, value in enumerate(fine):
                    m_ref[index, part, level, pl.ds(offset, ROWS, stride=3), :] = value[:, lanes]
        if early_ref is not None:
            copies += write_group(o_ref, m_ref, group, index, sem)
    for copy in copies:
        copy.wait()


def struct(*shape):
    return jax.ShapeDtypeStruct(shape, F32)


VMEM = pl.BlockSpec(memory_space=pltpu.VMEM)
HBM = pl.BlockSpec(memory_space=pltpu.HBM)
FIELD = (GROUPS, MAIN, 2 * COLS)
RIM = (GROUPS, 8, 2 * COLS)


def call(kernel, name, ins, outs, scratch, out_specs=None):
    return pl.pallas_call(
        kernel,
        in_specs=ins,
        out_specs=out_specs or [VMEM] * len(outs),
        out_shape=outs,
        scratch_shapes=scratch,
        compiler_params=pltpu.CompilerParams(vmem_limit_bytes=VMEM_LIMIT),
        name=name,
    )


def pinned(value):
    return pltpu.with_memory_space_constraint(value, pltpu.HBM)


def edges(gradients):
    scratch = [pltpu.SemaphoreType.DMA((3,))]
    outs = [pltpu.VMEM((3, LEVELS, 3 * ROWS, COLS), F32)] + [struct(BAND, COLS)] * 2
    gradients = pinned(gradients)
    return call(edges_kernel, "edges", [HBM], outs, scratch)(gradients)


def restrict(fine, ritz_vectors):
    scratch = [
        pltpu.VMEM((2 * BLOCK, 3 * COLS), BF16),
        pltpu.VMEM((HALO, 3 * COLS), F32),
        pltpu.VMEM((COLS, COLS), F32),
        pltpu.SemaphoreType.DMA((RITZ // PIECE,)),
    ]
    outs = [pltpu.VMEM((RITZ * MAIN, COLS), F32)]
    outs += [struct(*FIELD), struct(*RIM)] + [struct(RITZ, COLS)] * 2
    outs += [pltpu.VMEM((3 * COLS, 2 * COLS), BF16)]
    flat = pinned(ritz_vectors.reshape(RITZ * MAIN, COLS))
    return call(restrict_kernel, "restrict", [VMEM, HBM], outs, scratch)(fine, flat)


def sides(*args):
    outs = [struct(SIDE, COLS)] * 2 + [struct(*FIELD), struct(*RIM)] + [struct(MAIN + 8, COLS)] * 4
    return call(sides_kernel, "sides", [VMEM] * 7, outs, [pltpu.VMEM((COLS, COLS), F32)])(*args)


def bands(*args):
    return call(bands_kernel, "bands", [VMEM] * 3, [struct(EDGE + 8, COLS)] * 2, [])(*args)


def near(held, blocks, columns):
    outs, scratch = [struct(2, RITZ)], [pltpu.VMEM((2 * COLS, COLS), F32)]
    return call(near_kernel, "near", [VMEM] * 5, outs, scratch)(held, *blocks, *columns)[0]


def far(sums, held, blocks, columns):
    outs, scratch = [struct(GROUPS, RITZ)], [pltpu.VMEM((2 * COLS, COLS), F32)]
    return call(far_kernel, "far", [VMEM] * 6, outs, scratch)(sums, held, *blocks, *columns)[0]


def update(coefficients, ritz_vectors, messages):
    outs = [pltpu.VMEM((RITZ, 2, MAIN // 2, COLS), F32), struct(GROUPS * RITZ, COLS), struct(HALO, COLS)]
    outs += [struct(BLOCK, COLS)] * 3
    scratch = [pltpu.SemaphoreType.DMA((2, RITZ // CHUNK))]
    doubled = jnp.concatenate([coefficients, coefficients], axis=0)
    return call(update_kernel, "update", [VMEM, HBM] + [VMEM] * 4, outs, scratch)(
        doubled, pinned(ritz_vectors.reshape(RITZ, 2, MAIN // 2, COLS)), *messages
    )


def own(*args):
    return call(own_kernel, "own", [VMEM] * 3, [struct(BLOCK, COLS)], [])(*args)[0]


def prolong(slots, returned, main, edge, left, right, early=None):
    scratch = [
        pltpu.VMEM((BLOCK, 2 * COLS), F32),
        pltpu.VMEM((BLOCK, 3 * COLS), F32),
        pltpu.VMEM((2 * COLS, 3 * COLS), BF16),
    ]
    stage = (2, 3, DEPTH, 3 * ROWS, COLS)
    args = (*returned, main, edge, left, right)
    specs = [VMEM] * 6
    kernel = functools.partial(prolong_kernel, slots)
    if early is None:
        return call(kernel, "prolong_early", specs, [pltpu.VMEM(stage, F32)], scratch)(*args)[0]
    scratch += [pltpu.VMEM(stage, F32), pltpu.SemaphoreType.DMA((2, 3)), pltpu.SemaphoreType.DMA((2, 3))]
    outs = [jax.ShapeDtypeStruct((GROUPS * DEPTH, 3 * ROWS, 3 * COLS), F32)]
    return call(kernel, "prolong_late", specs + [VMEM], outs, scratch, [HBM])(*args, early)[0]


def exchange_members(blocks):
    size = lax.axis_size("mem")
    order = (2, 3, 1)
    sent = {shift: lax.ppermute(blocks[shift], "mem", [(i, i ^ shift) for i in range(size)]) for shift in order}
    return [sent[shift] for shift in range(1, size)]


def exchange_sum(value, axes):
    size = lax.axis_size(axes)
    copies = jnp.broadcast_to(value[None], (size,) + value.shape)
    return jnp.sum(lax.all_to_all(copies, axes, 0, 0, tiled=True), axis=0)


def per_device(gradients, ritz_vectors, ritz_values):
    lats, lons = lax.axis_size("lat"), lax.axis_size("lon")

    gradients = gradients.reshape(gradients.shape[1:])
    fine, down, up = edges(gradients)
    over = [(i, (i + 1) % lats) for i in range(lats)]
    under = [((i + 1) % lats, i) for i in range(lats)]
    above = lax.ppermute(down, "lat", over)
    below = lax.ppermute(up, "lat", under)
    held, main, edge, first, last, weights = restrict(fine, ritz_vectors)
    to_left, to_right, main, edge, *blocks = sides(above, below, main, edge, first, last, weights)
    right = lax.ppermute(to_left, "lon", [((i + 1) % lons, i) for i in range(lons)])
    left = lax.ppermute(to_right, "lon", [(i, (i + 1) % lons) for i in range(lons)])
    spread = [blocks[0]] + exchange_members(blocks)
    near_sums = near(held, (spread[0], spread[2]), (left, right))
    left, right, near_sums, *spread = lax.optimization_barrier((left, right, near_sums, *spread))
    down, up = bands(held, left, right)
    above = lax.ppermute(down, "lat", over)
    below = lax.ppermute(up, "lat", under)
    *spread, _, _ = lax.optimization_barrier((*spread, down, up))
    partial = far(near_sums, held, (spread[3], spread[1]), (left, right))
    cells = GROUPS * DEPTH * ROWS * lats * COLS * lons
    factors = (1.0 / ritz_values - 1.0) * (1.0 / cells)
    partial, factors = lax.optimization_barrier((partial, factors))
    for shift in (1, 2):
        partial = partial + lax.ppermute(partial, "mem", [(i, i ^ shift) for i in range(4)])
    coefficients = factors[None, :] * exchange_sum(partial, ("lat", "lon"))
    messages = (above, below, left, right)
    held, weights, own_edge, *sent = update(coefficients, ritz_vectors, messages)
    returned = exchange_members([None] + sent)
    mine = own(held, weights, own_edge)
    returned = [mine] + returned
    early = prolong(EARLY, [returned[slot] for slot in EARLY], main, edge, left, right)
    output = prolong(LATE, [returned[slot] for slot in LATE], main, edge, left, right, early)
    preconditioned = output[None]
    return preconditioned, coefficients


def solution(mesh):
    placed = (P("mem", None, "lat", "lon"), P(None, "mem", "lat", "lon"), P())
    return jax.shard_map(
        per_device,
        mesh=mesh,
        in_specs=placed,
        out_specs=(P("mem", None, "lat", "lon"), P()),
        check_vma=False,
    )
```
